32 devices in a mesh: page: 8 (over z, x), band: 4 (over y, core).
Axes of the slice: x: 2, y: 2, z: 4, core: 2. Of those that a mesh axis runs over, the one named last changes fastest.
Arguments:
- hidden: bfloat16 [32768, 768], P(('page', 'band')), may hold values from -6 to 6
- page_ids: int32 [32768], P(('page', 'band')), may hold values from 0 to 1, as said below
- key_mask: int32 [32768], P(('page', 'band')), may hold values from 0 to 1, as said below
- out_grad: bfloat16 [32768, 768], P(('page', 'band')), may hold values from -6 to 6
- w_query: bfloat16 [768, 768], replicated, may hold values from -0.4375 to 0.4375
- b_query: float32 [768], replicated, may hold values from -3 to 3
- w_key: bfloat16 [768, 768], replicated, may hold values from -0.21875 to 0.21875
- w_value: bfloat16 [768, 768], replicated, may hold values from -0.21875 to 0.21875
- b_value: float32 [768], replicated, may hold values from -3 to 3
- w_out: bfloat16 [768, 768], replicated, may hold values from -0.875 to 0.875
- b_out: float32 [768], replicated, may hold values from -3 to 3
- gain_one: float32 [768], replicated, may hold values from 0.5 to 1.5
- shift_one: float32 [768], replicated, may hold values from -2 to 2
- w_up: bfloat16 [768, 3072], replicated, may hold values from -0.21875 to 0.21875
- b_up: float32 [3072], replicated, may hold values from -3 to 3
- w_down: bfloat16 [3072, 768], replicated, may hold values from -0.109375 to 0.109375
- b_down: float32 [768], replicated, may hold values from -2 to 2
- gain_two: float32 [768], replicated, may hold values from 0.5 to 1.5
- shift_two: float32 [768], replicated, may hold values from -2 to 2
Outputs:
- output: bfloat16 [32768, 768], P(('page', 'band'))
- input_grad: bfloat16 [32768, 768], P(('page', 'band'))
- grad_w_query: float32 [768, 768], replicated
- grad_b_query: float32 [768], replicated
- grad_w_key: float32 [768, 768], replicated
- grad_w_value: float32 [768, 768], replicated
- grad_b_value: float32 [768], replicated
- grad_w_out: float32 [768, 768], replicated
- grad_b_out: float32 [768], replicated
- grad_gain_one: float32 [768], replicated
- grad_shift_one: float32 [768], replicated
- grad_w_up: float32 [768, 3072], replicated
- grad_b_up: float32 [3072], replicated
- grad_w_down: float32 [3072, 768], replicated
- grad_b_down: float32 [768], replicated
- grad_gain_two: float32 [768], replicated
- grad_shift_two: float32 [768], replicated
The draws below stay inside these ranges and needn't reach their ends.
Inputs may be any that keep to these rules, and one draw needn't show every extreme that they name: Within each block of 1024 slots the slots with key_mask 1 come first; 32768 // 1024 blocks in all, and some block is full of them in every draw. `page_ids`: document within its document group; within a block the slots with key_mask 1 are in order of document, and every document of the group has such slots in every block of the group.
All inputs are finite; a program needn't handle non-finite values.
Results may differ from the reference program's by a relative error of at most 0.015.
The reference program's roundings to bfloat16 on the way count: a program that leaves them out, or rounds other values in their place, can miss the bound.
Values may be sent and summed in bfloat16 or wider, within the bound.
No kernel may reach another device: no remote copies, remote signals or barrier semaphores. Data moves between devices by JAX's collectives and lax.ppermute only.
A program may use at most 256 MiB of HBM per device.

```python
import jax
import jax.numpy as jnp
from jax import lax

D = 768
HEADS = 12
HEAD = 64
FF = 3072
CAP = 1024
PAGES = 2
ROWS = 32768
N_PAGE = 8
N_BAND = 4


def band_layout(key):
    devices = ROWS // CAP
    count_key, full_key, cut_key, filler_key = jax.random.split(key, 4)
    counts = jax.random.randint(count_key, (devices,), CAP // 2, CAP + 1)
    fullest = jax.random.randint(full_key, (), 0, devices)
    counts = jnp.where(jnp.arange(devices) == fullest, CAP, counts)
    stride_index = jnp.arange(1, PAGES)
    offsets = jax.random.randint(cut_key, (devices, PAGES - 1), 1, 4)
    bounds = counts[:, None] * (4 * stride_index[None, :] + offsets) // (4 * PAGES)
    places = jnp.arange(CAP)
    page_rank = jnp.sum((places[None, :, None] >= bounds[:, None, :]).astype(jnp.int32), axis=2)
    filler = jax.random.randint(filler_key, (devices, CAP), 0, PAGES)
    active_rows = places[None, :] < counts[:, None]
    page_values = jnp.where(active_rows, page_rank, filler).astype(jnp.int32).reshape(ROWS)
    return (page_values, active_rows.astype(jnp.int32).reshape(ROWS))


def draw_page_ids(key, part):
    layout = band_layout(key)
    return layout[0]


def draw_key_mask(key, part):
    layout = band_layout(key)
    return layout[1]


def levels(own_key, dims, cuts, smallest, high):
    factor_of, own = 1.0, jax.random.fold_in(own_key, 6)
    for axis_at, shards_of in cuts:
        draws = jnp.exp(jax.random.uniform(jax.random.fold_in(own, axis_at), (shards_of,), jnp.float32, smallest / len(cuts), high / len(cuts)))
        factor_of = factor_of * jnp.repeat(draws, dims[axis_at] // shards_of).reshape([-1 if axis == axis_at else 1 for axis in range(len(dims))])
    return factor_of


def bell_draw(own_key, extent, deviation, reach, cuts=(), kind=jnp.bfloat16):
    values = jax.random.normal(own_key, extent, jnp.float32) * deviation
    if len(cuts) > 0:
        values = levels(own_key, extent, cuts, -0.22, 0.18) * values
    return jnp.clip(values, min=-reach, max=reach).astype(kind)


def setup_inputs(seed: int = 0) -> dict:
    seeds = jax.random.split(jax.random.key(seed), 20)
    return {
        "hidden": bell_draw(seeds[0], (ROWS, D), 1.0, 6.0, ((0, 32),)),
        "page_ids": draw_page_ids(jax.random.fold_in(seeds[19], 71), 0),
        "key_mask": draw_key_mask(jax.random.fold_in(seeds[19], 71), 0),
        "out_grad": bell_draw(seeds[3], (ROWS, D), 1.0, 6.0, ((0, 32),)),
        "w_query": bell_draw(seeds[4], (D, D), (D // 4) ** -0.5, 0.4375),
        "b_query": bell_draw(seeds[5], (D,), 0.5, 3.0, (), jnp.float32),
        "w_key": bell_draw(seeds[6], (D, D), D ** -0.5, 0.21875),
        "w_value": bell_draw(seeds[7], (D, D), D ** -0.5, 0.21875),
        "b_value": bell_draw(seeds[8], (D,), 0.5, 3.0, (), jnp.float32),
        "w_out": bell_draw(seeds[9], (D, D), (D // 16) ** -0.5, 0.875),
        "b_out": bell_draw(seeds[10], (D,), 0.5, 3.0, (), jnp.float32),
        "gain_one": jnp.clip(1.0 + 0.1 * jax.random.normal(seeds[11], (D,), jnp.float32), 0.5, 1.5),
        "shift_one": bell_draw(seeds[12], (D,), 0.3, 2.0, (), jnp.float32),
        "w_up": bell_draw(seeds[13], (D, FF), D ** -0.5, 0.21875),
        "b_up": bell_draw(seeds[14], (FF,), 0.5, 3.0, (), jnp.float32),
        "w_down": bell_draw(seeds[15], (FF, D), FF ** -0.5, 0.109375),
        "b_down": bell_draw(seeds[16], (D,), 0.3, 2.0, (), jnp.float32),
        "gain_two": jnp.clip(1.0 + 0.1 * jax.random.normal(seeds[17], (D,), jnp.float32), 0.5, 1.5),
        "shift_two": bell_draw(seeds[18], (D,), 0.3, 2.0, (), jnp.float32),
    }


@jax.custom_vjp
def low(v):
    return lax.optimization_barrier(v.astype(jnp.bfloat16)).astype(jnp.float32)

@jax.custom_vjp
def low_back(v):
    return v

def low_keep(v):
    return (low(v), None)

def low_pass(kept, grad):
    return (grad,)

def back_keep(v):
    return (v, None)

def back_low(kept, grad):
    return (low(grad),)
low.defvjp(low_keep, low_pass)
low_back.defvjp(back_keep, back_low)

def both_round(value):
    return low(low_back(value))

def product(left, right):
    return jnp.dot(left, right, precision=lax.Precision.HIGHEST)

def norm_rows(values, gain, shift):
    centre = lax.optimization_barrier(jnp.mean(values, axis=-1, keepdims=True))
    centred = values - centre
    spread = lax.optimization_barrier(jnp.mean(centred * centred, axis=-1, keepdims=True))
    return centred * lax.rsqrt(spread + 1e-12) * gain + shift

def reference(hidden, page_ids, key_mask, out_grad, w_query, b_query, w_key, w_value, b_value, w_out, b_out, gain_one, shift_one, w_up, b_up, w_down, b_down, gain_two, shift_two):
    blocks = N_PAGE * N_BAND
    key_tags = jnp.where(key_mask == 1, page_ids + 1, 0).astype(jnp.int32).reshape(N_PAGE, N_BAND, CAP)
    tag_pad = jnp.pad(key_tags, ((0, 0), (1, 1), (0, 0)))
    query_tags = (page_ids + 1).astype(jnp.int32).reshape(blocks, CAP)
    params = tuple((member.astype(jnp.float32) for member in (w_query, b_query, w_key, w_value, b_value, w_out, b_out, gain_one, shift_one, w_up, b_up, w_down, b_down, gain_two, shift_two)))
    inputs = hidden.astype(jnp.float32)
    cotangent = out_grad.astype(jnp.float32) * key_mask.astype(jnp.float32)[:, None]

    def forward(source, wq_mat, bq_vec, wk_mat, wv_mat, bv_vec, wo_mat, bo_vec, gain_a, shift_a, wu_mat, bu_vec, wd_mat, bd_vec, gain_b, shift_b):
        queries = both_round(product(source, wq_mat) + bq_vec)
        key_rows = both_round(product(source, wk_mat))
        value_rows = both_round(product(source, wv_mat) + bv_vec)
        key_pad = jnp.pad(key_rows.reshape(N_PAGE, N_BAND, CAP, D), ((0, 0), (1, 1), (0, 0), (0, 0)))
        value_pad = jnp.pad(value_rows.reshape(N_PAGE, N_BAND, CAP, D), ((0, 0), (1, 1), (0, 0), (0, 0)))
        query_blocks = queries.reshape(blocks, CAP, D)

        def attend(device):
            group = device // N_BAND
            band_index = device % N_BAND
            anchor = jnp.zeros((), jnp.int32)
            near_keys = lax.dynamic_slice(key_pad, (group, band_index, anchor, anchor), (1, 3, CAP, D)).reshape(3 * CAP, HEADS, HEAD)
            near_values = lax.dynamic_slice(value_pad, (group, band_index, anchor, anchor), (1, 3, CAP, D)).reshape(3 * CAP, HEADS, HEAD)
            near_tags = lax.dynamic_slice(tag_pad, (group, band_index, anchor), (1, 3, CAP)).reshape(3 * CAP)
            own_query = lax.dynamic_index_in_dim(query_blocks, device, 0, keepdims=False).reshape(CAP, HEADS, HEAD)
            own_tags = lax.dynamic_index_in_dim(query_tags, device, 0, keepdims=False)
            allowed = own_tags[:, None] == near_tags[None, :]
            scores = low_back(jnp.einsum('ihd,jhd->hij', own_query, near_keys, precision=lax.Precision.HIGHEST) * HEAD ** (-0.5))
            masked = jnp.where(allowed[None], scores, -1e+30)
            probs = low(jax.nn.softmax(masked, axis=-1))
            mixed = jnp.einsum('hij,jhd->ihd', probs, near_values, precision=lax.Precision.HIGHEST)
            return both_round(mixed.reshape(CAP, D))
        mixed_all = lax.map(jax.checkpoint(attend), jnp.arange(blocks, dtype=jnp.int32)).reshape(blocks * CAP, D)
        attention = low_back(product(mixed_all, wo_mat) + bo_vec)
        normed_one = norm_rows(source + attention, gain_a, shift_a)
        upper_in = low_back(product(low(normed_one), wu_mat) + bu_vec)
        active = low(jax.nn.gelu(upper_in, approximate=False))
        branch = low_back(product(active, wd_mat) + bd_vec)
        return norm_rows(normed_one + branch, gain_b, shift_b)
    result, pullback = jax.vjp(forward, inputs, *params)
    grads = pullback(cotangent)
    return (result.astype(jnp.bfloat16), grads[0].astype(jnp.bfloat16), grads[1], grads[2], grads[3], grads[4], grads[5], grads[6], grads[7], grads[8], grads[9], grads[10], grads[11], grads[12], grads[13], grads[14], grads[15])
```

```python
import functools

import jax
import jax.numpy as jnp
from jax import lax
from jax.experimental import pallas as pl
from jax.experimental.pallas import tpu as pltpu
from jax.sharding import PartitionSpec as P


HEAD = 64
PAIR = 128
BLOCKED = -1e30
SAFE = 60.0
NT = (((1,), (1,)), ((), ()))
NN = (((1,), (0,)), ((), ()))
TN = (((0,), (0,)), ((), ()))
F32 = jnp.float32
BF16 = jnp.bfloat16
SCALE = HEAD**-0.5
TILE = 256


def mm(a, b, dims):
    return lax.dot_general(a, b, dims, preferred_element_type=F32)


def col_sum(x):
    return jnp.sum(x, axis=0, keepdims=True)


def tile_at(i, tile=TILE):
    return pl.ds(pl.multiple_of(i * tile, tile), tile)


def parts(x):
    hi = x.astype(BF16)
    rest = x - hi.astype(F32)
    mid = rest.astype(BF16)
    return hi, mid, (rest - mid.astype(F32)).astype(BF16)


def same_half():
    a, b = (lax.broadcasted_iota(jnp.int32, (PAIR, PAIR), i) < HEAD for i in (0, 1))
    return jnp.where(a == b, 1.0, 0.0).astype(BF16)


def left_lanes():
    return lax.broadcasted_iota(jnp.int32, (1, PAIR), 1) < HEAD


def attend_kernel(keys, q_ref, k_ref, v_ref, qtag_ref, ktag_ref, o_ref, ext_ref, qx0, qx1, vt, acc0, acc1, top0, top1):
    rows, near = q_ref.shape[0], k_ref.shape[0]
    left = left_lanes()
    q_pair = q_ref[...] * jnp.asarray(SCALE, BF16)
    zero = jnp.zeros_like(q_pair)
    qx0[:, :PAIR] = jnp.where(left, q_pair, zero)
    qx1[:, :PAIR] = jnp.where(left, zero, q_pair)
    qx0[:, PAIR:] = qtag_ref[...]
    qx1[:, PAIR:] = qtag_ref[...]
    turned = v_ref[...].T
    vt[:HEAD, :] = turned[:HEAD]
    vt[HEAD:PAIR, :] = jnp.ones((HEAD, near), BF16)
    vt[PAIR:, :] = turned[HEAD:]
    heads = ((acc0, top0, qx0, slice(0, PAIR)), (acc1, top1, qx1, slice(HEAD, HEAD + PAIR)))
    for acc, *_ in heads:
        acc[...] = jnp.zeros_like(acc)
    halves = same_half()

    def longest(x):
        x = x.astype(F32)
        return jnp.max(mm((x * x).astype(BF16), halves, NN), axis=0, keepdims=True)

    plain = jnp.max(longest(k_ref[...]) * longest(q_pair)) < (SAFE * 0.98) ** 2
    key_side = lambda ks: jnp.concatenate([k_ref[ks, :], ktag_ref[ks, :]], axis=1)

    @pl.when(plain)
    def _():
        for _, top, *_ in heads:
            top[...] = jnp.zeros_like(top)
        for band in range(near // rows):
            for n in range(1, rows // TILE + 1):
                @pl.when(keys[band] == n)
                def _():
                    ks = pl.ds(band * rows, n * TILE)
                    kx = key_side(ks)
                    for acc, _, qx, at in heads:
                        p = jnp.exp(mm(kx, qx[...], NT)).astype(BF16)
                        acc[...] += mm(vt[at, ks], p, NN)

    @pl.when(jnp.logical_not(plain))
    def _():
        for _, top, *_ in heads:
            top[...] = jnp.full_like(top, -3e38)

        def per_k(ki, _):
            @pl.when(lax.rem(ki, rows // TILE) < keys[lax.div(ki, rows // TILE)])
            def _():
                ks = tile_at(ki)
                kx = key_side(ks)
                for acc, top, qx, at in heads:
                    s = mm(kx, qx[...], NT)
                    old = top[...]
                    new = jnp.maximum(old, jnp.max(s, axis=0, keepdims=True))
                    p = jnp.exp(s - new[:1, :]).astype(BF16)
                    acc[...] = acc[...] * jnp.exp(old - new)[:1, :] + mm(vt[at, ks], p, NN)
                    top[...] = new
            return 0

        lax.fori_loop(0, near // TILE, per_k, 0)

    def finish(qi, _):
        qs = tile_at(qi)
        tags = qtag_ref[qs, :].astype(F32).T[:8]
        place = lax.broadcasted_iota(jnp.int32, (8, TILE), 0)
        out, ext = [], []
        for acc, top, _, at in heads:
            total, plain_out = (acc[HEAD:, qs], acc[:HEAD, qs]) if at.start == 0 else (acc[:HEAD, qs], acc[HEAD:, qs])
            out.append(plain_out / total)
            hi, mid, lo = (x.astype(F32) for x in parts(jnp.log(total[:8]) + top[:, qs]))
            head = jnp.where(place == 2, hi, jnp.where(place == 3, mid, jnp.where(place == 4, lo, tags)))
            ext += [head, jnp.zeros((HEAD - 8, TILE), F32)]
        o_ref[qs, :] = jnp.concatenate(out, axis=0).T.astype(BF16)
        ext_ref[qs, :] = jnp.concatenate(ext, axis=0).T.astype(BF16)
        return 0

    lax.fori_loop(0, rows // TILE, finish, 0)


def attend(q, k, v, qtag, ktag, keys):
    rows, d = q.shape
    near = k.shape[0]
    part = lambda n: pl.BlockSpec((n, PAIR), lambda p, *_: (0, p))
    fixed = lambda n: pl.BlockSpec((n, PAIR), lambda p, *_: (0, 0))
    return pl.pallas_call(
        attend_kernel,
        grid_spec=pltpu.PrefetchScalarGridSpec(
            num_scalar_prefetch=1,
            grid=(d // PAIR,),
            in_specs=[part(rows), part(near), part(near), fixed(rows), fixed(near)],
            out_specs=[part(rows)] * 2,
            scratch_shapes=[pltpu.VMEM((rows, 2 * PAIR), BF16)] * 2 + [pltpu.VMEM((PAIR + HEAD, near), BF16)]
            + [pltpu.VMEM((PAIR, rows), F32)] * 2 + [pltpu.VMEM((8, rows), F32)] * 2,
        ),
        out_shape=[jax.ShapeDtypeStruct((rows, d), BF16)] * 2,
        compiler_params=pltpu.CompilerParams(vmem_limit_bytes=56 * 2**20),
        cost_estimate=pl.CostEstimate(flops=40 * 10**9, bytes_accessed=16 * 2**20, transcendentals=0),
        name="attend",
    )(keys, q, k, v, qtag, ktag)


def hull(qbits, want, nq):
    first, last = jnp.int32(nq), jnp.int32(0)
    for qi in reversed(range(nq)):
        hit = (qbits[qi] & want) != 0
        last = jnp.where(hit & (last == 0), qi + 1, last)
        first = jnp.where(hit, qi, first)
    return first, jnp.maximum(last - first, 0)


def attend_back_kernel(tk, qbits, kbits, q_ref, k_ref, v_ref, g_ref, o_ref, ext_ref, ktag_ref, near_ref, *refs):
    dq_ref, dk_ref, dv_ref, sums, w_ref, qx0, qx1, gx0, gx1, qt, gt, dq_acc, dk_acc, dv_acc = refs[-14:]
    rows, near = q_ref.shape[0], k_ref.shape[0]
    nq = rows // TILE
    left = left_lanes()
    place = lax.broadcasted_iota(jnp.int32, (1, PAIR), 1) % HEAD
    halves = same_half()

    def per_q(qi, _):
        qs = tile_at(qi)
        q_pair, g_pair, ext = q_ref[qs, :], g_ref[qs, :], ext_ref[qs, :]
        qt[:, qs] = q_pair.T
        gt[:, qs] = g_pair.T
        zero = jnp.zeros_like(q_pair)
        hi, mid, _ = parts(g_pair.astype(F32) * o_ref[qs, :].astype(F32))
        hi, mid, _ = parts(mm(hi, halves, NN) + mm(mid, halves, NN))
        inner = jnp.where(place == 2, hi, jnp.where(place == 3, mid, zero))
        scaled = q_pair * jnp.asarray(SCALE, BF16)
        for x0, x1, base, more in ((qx0, qx1, scaled, ext), (gx0, gx1, g_pair, inner)):
            x0[qs, :PAIR] = jnp.where(left, base, zero)
            x1[qs, :PAIR] = jnp.where(left, zero, base)
            x0[qs, PAIR:] = jnp.where(left, more, zero)
            x1[qs, PAIR:] = jnp.where(left, zero, more)
        return 0

    lax.fori_loop(0, nq, per_q, 0)
    dq_acc[...] = jnp.zeros_like(dq_acc)

    def per_k(ki, _):
        first, count = hull(qbits, kbits[ki], nq)
        ks = tile_at(ki, tk)

        @pl.when(count == 0)
        def _():
            dk_acc[:, ks] = jnp.zeros((PAIR, tk), F32)
            dv_acc[:, ks] = jnp.zeros((PAIR, tk), F32)

        for n in range(1, nq + 1):
            @pl.when(count == n)
            def _():
                qs = pl.ds(pl.multiple_of(first * TILE, TILE), n * TILE)
                k_pair, tags = k_ref[ks, :], ktag_ref[ks, :]
                zero = jnp.zeros_like(k_pair)
                kx = jnp.concatenate([k_pair, tags], axis=1)
                vx = jnp.concatenate([v_ref[ks, :], tags], axis=1)
                dq = 0.0
                for qx, gx, at, kz in ((qx0, gx0, 0, jnp.where(left, k_pair, zero)),
                                       (qx1, gx1, HEAD, jnp.where(left, zero, k_pair))):
                    head = slice(at, at + HEAD)
                    p = jnp.exp(mm(qx[qs, :], kx, NT))
                    ds = (p * mm(gx[qs, :], vx, NT)).astype(BF16)
                    dv_acc[head, ks] = mm(gt[head, qs], p.astype(BF16), NN)
                    dk_acc[head, ks] = mm(qt[head, qs], ds, NN)
                    dq = dq + mm(ds, kz, NN)
                dq_acc[qs, :] += dq
        return 0

    lax.fori_loop(0, near // tk, per_k, 0)
    dq = (dq_acc[...] * SCALE).astype(BF16)
    dk = (dk_acc[...] * SCALE).astype(BF16)
    dv = dv_acc[...].astype(BF16)
    dq_ref[...] = dq
    dk_ref[...] = dk.T
    dv_ref[...] = dv.T
    w_ref[:, :PAIR] = mm(dq, near_ref[:rows, :], TN).T
    w_ref[:, PAIR:2 * PAIR] = mm(dk, near_ref[...], NN).T
    w_ref[:, 2 * PAIR:] = mm(dv, near_ref[...], NN).T
    sums[0:1, :] = col_sum(dq_ref[...].astype(F32))
    sums[1:2, :] = mm(jnp.ones((8, near), BF16), dv_ref[...], NN)[:1]
    sums[2:, :] = jnp.zeros((6, PAIR), F32)


def attend_back(pair, pairs, kept, after, q, k, v, g, o, ext, ktag, near_rows, qbits, kbits, tk):
    rows, d = q.shape
    near = k.shape[0]
    part = lambda n: pl.BlockSpec((n, PAIR), lambda p, *_: (0, pair + p))
    hold = pl.BlockSpec(memory_space=pl.ANY)
    extra = list(kept) + list(after)
    return pl.pallas_call(
        functools.partial(attend_back_kernel, tk),
        grid_spec=pltpu.PrefetchScalarGridSpec(
            num_scalar_prefetch=2,
            grid=(pairs,),
            in_specs=[part(rows), part(near), part(near)] + [part(rows)] * 3 + [pl.BlockSpec((near, PAIR), lambda p, *_: (0, 0)),
               pl.BlockSpec((near, d), lambda p, *_: (0, 0), pipeline_mode=pl.Buffered(1))]
            + [hold] * len(extra),
            out_specs=[part(rows), part(near), part(near), pl.BlockSpec((8, PAIR), lambda p, *_: (0, p)),
                       pl.BlockSpec((d, 3 * PAIR), lambda p, *_: (0, p))],
            scratch_shapes=[pltpu.VMEM((rows, 2 * PAIR), BF16)] * 4 + [pltpu.VMEM((PAIR, rows), BF16)] * 2
            + [pltpu.VMEM((rows, PAIR), F32)] + [pltpu.VMEM((PAIR, near), F32)] * 2,
        ),
        out_shape=[jax.ShapeDtypeStruct((n, d), BF16) for n in (rows, near, near)]
        + [jax.ShapeDtypeStruct((8, pairs * PAIR), F32), jax.ShapeDtypeStruct((d, pairs * 3 * PAIR), F32)],
        input_output_aliases={10 + i: i for i in range(len(kept))},
        compiler_params=pltpu.CompilerParams(vmem_limit_bytes=56 * 2**20),
        cost_estimate=pl.CostEstimate(flops=18 * pairs * 10**9, bytes_accessed=8 * 2**20, transcendentals=0),
        name="attend_back",
    )(qbits, kbits, q, k, v, g, o, ext, ktag, near_rows, *extra)


def row_norm(values):
    centred = values - jnp.mean(values, axis=-1, keepdims=True)
    rstd = lax.rsqrt(jnp.mean(centred * centred, axis=-1, keepdims=True) + 1e-12)
    return centred * rstd, rstd


def norm_back(cot, gain, normed, rstd):
    e = cot * gain
    return rstd * (e - jnp.mean(e, axis=-1, keepdims=True) - normed * jnp.mean(e * normed, axis=-1, keepdims=True))


def dense_kernel(tf, hidden, mixed, out_grad, mask, w_out, w_up, w_down, b_out, gain_one, shift_one, b_up, b_down,
                 gain_two, shift_two, result, low_out, active, d_branch, d_upper, d_one, d_att, d_mixed, sums, sum_up,
                 slope):
    ff = w_up.shape[1]

    @pl.when(pl.program_id(0) == 0)
    def _():
        sums[...] = jnp.zeros_like(sums)
        sum_up[...] = jnp.zeros_like(sum_up)

    vec = lambda ref: ref[...].reshape(1, -1)
    r1 = hidden[...].astype(F32) + (mm(mixed[...], w_out[...], NN) + vec(b_out))
    n1, s1 = row_norm(r1)
    normed_one = n1 * vec(gain_one) + vec(shift_one)
    low = normed_one.astype(BF16)
    low_out[...] = low
    branch = jnp.zeros_like(r1)
    bias = vec(b_up)
    for t in range(0, ff, tf):
        c = pl.ds(t, tf)
        u = mm(low, w_up[:, c], NN) + bias[:, t:t + tf]
        phi = 0.5 + 0.5 * lax.erf(u * (0.5**0.5))
        a = (u * phi).astype(BF16)
        active[:, c] = a
        slope[:, c] = phi + u * (jnp.exp(u * u * -0.5) * 0.3989422804014327)
        branch = branch + mm(a, w_down[c, :], NN)
    n2, s2 = row_norm(normed_one + (branch + vec(b_down)))
    result[...] = (n2 * vec(gain_two) + vec(shift_two)).astype(BF16)
    cot = out_grad[...].astype(F32) * mask[...]
    d_two = norm_back(cot, vec(gain_two), n2, s2)
    db = d_two.astype(BF16)
    d_branch[...] = db
    sums[0:1, :] += col_sum(cot * n2)
    sums[1:2, :] += col_sum(cot)
    sums[2:3, :] += col_sum(db.astype(F32))
    d_normed = d_two
    for t in range(0, ff, tf):
        c = pl.ds(t, tf)
        du = (mm(db, w_down[c, :], NT) * slope[:, c]).astype(BF16)
        d_upper[:, c] = du
        sum_up[:, c] += col_sum(du.astype(F32))
        d_normed = d_normed + mm(du, w_up[:, c], NT)
    sums[3:4, :] += col_sum(d_normed * n1)
    sums[4:5, :] += col_sum(d_normed)
    d1 = norm_back(d_normed, vec(gain_one), n1, s1)
    d_one[...] = d1
    da = d1.astype(BF16)
    d_att[...] = da
    sums[5:6, :] += col_sum(da.astype(F32))
    d_mixed[...] = mm(da, w_out[...], NT).astype(BF16)


def dense(hidden, mixed, out_grad, mask, w_out, w_up, w_down, b_out, gain_one, shift_one, b_up, b_down, gain_two,
          shift_two, tr=256, tf=768):
    rows, d = hidden.shape
    ff = w_up.shape[1]
    row = lambda n: pl.BlockSpec((tr, n), lambda i: (i, 0))
    whole = lambda a, b: pl.BlockSpec((a, b), lambda i: (0, 0), pipeline_mode=pl.Buffered(1))
    flat = lambda n: pl.BlockSpec((n,), lambda i: (0,))
    shape = jax.ShapeDtypeStruct
    low = shape((rows, d), BF16)
    return pl.pallas_call(
        functools.partial(dense_kernel, tf),
        grid=(rows // tr,),
        in_specs=[row(d), row(d), row(d), row(1), whole(d, d), whole(d, ff), whole(ff, d), flat(d), flat(d), flat(d),
                  flat(ff), flat(d), flat(d), flat(d)],
        out_specs=[row(d), row(d), row(ff), row(d), row(ff), row(d), row(d), row(d),
                   pl.BlockSpec((8, d), lambda i: (0, 0)), pl.BlockSpec((1, ff), lambda i: (0, 0))],
        out_shape=[low, low, shape((rows, ff), BF16), low, shape((rows, ff), BF16), shape((rows, d), F32), low, low,
                   shape((8, d), F32), shape((1, ff), F32)],
        scratch_shapes=[pltpu.VMEM((tr, ff), F32)],
        compiler_params=pltpu.CompilerParams(vmem_limit_bytes=56 * 2**20),
        cost_estimate=pl.CostEstimate(flops=40 * 10**9, bytes_accessed=40 * 2**20, transcendentals=0),
        name="dense",
    )(hidden, mixed, out_grad, mask.astype(F32).reshape(-1, 1), w_out, w_up, w_down, b_out, gain_one, shift_one, b_up,
      b_down, gain_two, shift_two)


def back_kernel(dk, dv, w_key, w_value, *refs):
    total = mm(dk[...], w_key[...], NT) + mm(dv[...], w_value[...], NT)
    if len(refs) > 1:
        dq, w_query, kept = refs[:3]
        total = total + mm(dq[...], w_query[...], NT) + kept[...]
    refs[-1][...] = total.astype(refs[-1].dtype)


def back_product(start, rows, dk, dv, w_key, w_value, own=()):
    d = w_key.shape[0]
    tr = 512
    at = lambda i: (start // tr + i, 0)
    row = lambda place: pl.BlockSpec((tr, d), place)
    whole = pl.BlockSpec((d, d), lambda i: (0, 0))
    return pl.pallas_call(
        back_kernel,
        grid=(rows // tr,),
        in_specs=[row(at), row(at), whole, whole] + ([row(lambda i: (i, 0)), whole, row(lambda i: (i, 0))] if own else []),
        out_specs=row(lambda i: (i, 0)),
        out_shape=jax.ShapeDtypeStruct((rows, d), F32 if own else BF16),
        compiler_params=pltpu.CompilerParams(vmem_limit_bytes=40 * 2**20),
        cost_estimate=pl.CostEstimate(flops=(6 if own else 4) * rows * d * d, bytes_accessed=10 * rows * d, transcendentals=0),
        name="back_product",
    )(dk, dv, w_key, w_value, *own)


ALL = ("page", "band")


def everyone():
    return lax.axis_size("page") * lax.axis_size("band")


def swapped(block, mask):
    return lax.ppermute(block, ALL, [(i, i ^ mask) for i in range(everyone())])


def side(bit):
    return lax.rem(lax.div(lax.axis_index(ALL), bit), 2)


def masks_of(bits):
    masks = [0]
    for bit in reversed(bits):
        masks = masks + [mask | bit for mask in masks]
    return masks


def place_of(bits):
    at = 0
    for bit in bits:
        at = 2 * at + side(bit)
    return at


class Summing:
    def __init__(self, block, stages):
        self.stages, self.at = stages, 0
        self.deal(block)

    def deal(self, block):
        masks = masks_of(self.stages[self.at])
        rows = block.shape[0] // len(masks)
        place = place_of(self.stages[self.at])
        part = lambda i: lax.dynamic_slice_in_dim(block, jnp.bitwise_xor(place, i) * rows, rows)
        self.mine = part(0)
        self.others = [part(i).astype(BF16) for i in range(1, len(masks))]

    def advance(self, held=None):
        if self.at < len(self.stages):
            masks = masks_of(self.stages[self.at])
            theirs = [swapped(other, mask) for other, mask in zip(self.others, masks[1:])]
            if held is not None:
                theirs, held = lax.optimization_barrier((theirs, held))
            block = self.mine
            for other in theirs:
                block = block + other.astype(F32)
            self.at += 1
            if self.at < len(self.stages):
                self.deal(block)
            else:
                self.others = [block.astype(BF16)]
        return held

    def finish(self):
        while self.at < len(self.stages):
            self.advance()
        return self.others[0]


def hand_out(block, stages):
    for bits in reversed(stages):
        parts = [block] + [swapped(block, mask) for mask in masks_of(bits)[1:]]
        for i, bit in enumerate(bits):
            far = 1 << (len(bits) - 1 - i)
            flip = side(bit) == 1
            parts = [jnp.where(flip, parts[j ^ far], parts[j]) for j in range(len(parts))]
        block = jnp.concatenate(parts)
    return block


def added_up(vectors, stages):
    for bits in stages:
        parts = [vectors] + [swapped(vectors, mask) for mask in masks_of(bits)[1:]]
        while len(parts) > 1:
            parts = [parts[i] + parts[i + 1] for i in range(0, len(parts), 2)]
        vectors = parts[0]
    return vectors


def gather_all(blocks, orders):
    width = min(block.shape[1] for block in blocks)
    flat = [block[:, c:c + width] for block in blocks for c in range(0, block.shape[1], width)]
    got = lax.all_gather(jnp.concatenate(flat), ALL, axis=0, tiled=False)
    bits = [1 << i for i in reversed(range(everyone().bit_length() - 1))]
    out, at = [], 0
    for block, order in zip(blocks, orders):
        rows = block.shape[0]
        parts = []
        for _ in range(0, block.shape[1], width):
            part = got[:, at:at + rows].reshape([2] * len(bits) + [rows, width])
            part = part.transpose([bits.index(bit) for stage in order for bit in stage] + [len(bits), len(bits) + 1])
            parts.append(part.reshape(-1, width).astype(F32))
            at += rows
        out.append(jnp.concatenate(parts, axis=1))
    return out


def tag_columns(page_ids, near_tags):
    place = jnp.arange(PAIR)[None, :] % HEAD
    qtag = jnp.where(jnp.arange(PAIR)[None, :] == page_ids[:, None], 1.0, 0.0).astype(BF16)
    ktag = jnp.where((place < 2) & (near_tags[:, None] != place + 1), BLOCKED, 0.0)
    return qtag, jnp.where((place >= 2) & (place < 5), -1.0, ktag).astype(BF16)


def tokens_of(near_tags, rows):
    have = jnp.sum((near_tags.reshape(-1, rows) > 0).astype(jnp.int32), axis=1)
    return (have + (TILE - 1)) // TILE


def tile_bits(tags, tile):
    tags = tags.reshape(-1, tile)
    return sum(jnp.max(jnp.where(tags == d + 1, 1 << d, 0), axis=1) for d in range(2)).astype(jnp.int32)


def body(hidden, page_ids, key_mask, out_grad, w_query, b_query, w_key, w_value, b_value, w_out, b_out, gain_one,
         shift_one, w_up, b_up, w_down, b_down, gain_two, shift_two):
    rows, d = hidden.shape
    bands = lax.axis_size("band")
    mates = [(i, i ^ 1) for i in range(bands)]
    across = [(i, i + 1) for i in range(1, bands - 1, 2)] + [(i + 1, i) for i in range(1, bands - 1, 2)]
    to_mate = lambda x: lax.ppermute(x, "band", mates)
    to_across = lambda x: lax.ppermute(x, "band", across)

    key_tags = jnp.where(key_mask == 1, page_ids + 1, 0)
    far = to_across(hidden)
    mate = to_mate(hidden)
    near_tags = jnp.concatenate([key_tags, to_mate(key_tags), to_across(key_tags)])
    queries = (mm(hidden, w_query, NN) + b_query).astype(BF16)
    near = jnp.concatenate([hidden, mate, far])
    keys = mm(near, w_key, NN).astype(BF16)
    values = (mm(near, w_value, NN) + b_value).astype(BF16)
    qtag, ktag = tag_columns(page_ids, near_tags)

    mixed, ext = attend(queries, keys, values, qtag, ktag, tokens_of(near_tags, rows))
    (result, normed_low, active, d_branch, d_upper, d_one, d_att, d_mixed, sums, sum_up) = dense(
        hidden, mixed, out_grad, key_mask, w_out, w_up, w_down, b_out, gain_one, shift_one, b_up, b_down, gain_two,
        shift_two)

    count = everyone().bit_length() - 1
    core, y, x, z = 1, 2, bands, 2 * bands
    rest = [1 << i for i in range(count) if 1 << i not in (core, y, x, z)]
    turns = [[[core]] + [[bit] for bit in order + rest] for order in ([x, y, z], [y, z, x], [z, x, y])]
    direct = [[core], [x, y]] + [([z] + rest)[i:i + 2] for i in range(0, 1 + len(rest), 2)]

    cut = active.shape[1] * 3 // 4
    streams = [Summing(mm(active[:, :cut], d_branch, TN), turns[0])]
    streams.append(Summing(mm(normed_low, d_upper[:, :cut], TN), turns[1]))
    third = [mm(active[:, cut:], d_branch, TN), mm(normed_low, d_upper[:, cut:], TN), mm(mixed, d_att, TN)]
    streams.append(Summing(jnp.concatenate(third, axis=1), turns[2]))
    for stream in streams:
        d_mixed = stream.advance(d_mixed)
    after = [other for stream in streams for other in stream.others]

    tk = 512
    bits = (tile_bits(key_tags, TILE), tile_bits(near_tags, tk))
    pairs = d // PAIR
    kept, end_sums, groups, at, parts = (), [], [], 0, []
    for size in [1] * (pairs - 2) + [2]:
        *kept, part_sums, part = attend_back(at, size, kept, after, queries, keys, values, d_mixed, mixed, ext, ktag, near,
                                             *bits, tk)
        at += size
        end_sums.append(part_sums)
        parts.append(part)
        if at < pairs:
            after = []
            for stream in streams:
                kept[0] = stream.advance(kept[0])
                after = after + stream.others
        if at % 2 == 0:
            group = Summing(jnp.concatenate(parts, axis=1), direct)
            parts = []
            groups.append(group)
            streams = streams + [group]
            after = after + group.others
    dq, dk, dv = kept

    first, second, third = gather_all([stream.finish() for stream in streams[:3]], turns)
    grad_down = jnp.concatenate([first, third[:, :d]])
    grad_up = jnp.concatenate([second, third[:, d:2 * d]], axis=1)
    grad_out = third[:, 2 * d:]

    vectors = [sums, sum_up.reshape(-1, d)] + [jnp.concatenate([e[i:i + 1] for e in end_sums], axis=1) for i in (0, 1)]
    vectors = added_up(jnp.concatenate(vectors), direct)

    far_part = to_across(back_product(2 * rows, rows, dk, dv, w_key, w_value))
    mate_part = to_mate(back_product(rows, rows, dk, dv, w_key, w_value))
    own_part = back_product(0, rows, dk, dv, w_key, w_value, (dq, w_query, d_one))
    input_grad = (own_part + mate_part.astype(F32) + far_part.astype(F32)).astype(BF16)

    groups = [hand_out(group.finish(), direct).astype(F32).reshape(d, 2, 3, PAIR) for group in groups]
    grads = [jnp.concatenate([group[:, p, i] for group in groups for p in range(2)], axis=1) for i in range(3)]
    ups = 8 + sum_up.size // d
    return (
        result,
        input_grad,
        grads[0],
        vectors[ups],
        grads[1],
        grads[2],
        vectors[ups + 1],
        grad_out,
        vectors[5],
        vectors[3],
        vectors[4],
        grad_up,
        vectors[8:ups].reshape(-1),
        grad_down,
        vectors[2],
        vectors[0],
        vectors[1],
    )


def solution(mesh):
    split = P(("page", "band"), None)
    line = P(("page", "band"))
    return jax.shard_map(
        body,
        mesh=mesh,
        in_specs=(split, line, line, split) + (P(),) * 15,
        out_specs=(split, split) + (P(),) * 15,
        check_vma=False,
    )
```

```python
import functools

import jax
import jax.numpy as jnp
from jax import lax
from jax.experimental import pallas as pl
from jax.experimental.pallas import tpu as pltpu
from jax.sharding import PartitionSpec as P


HEAD = 64
PAIR = 128
BLOCKED = -1e30
SAFE = 60.0
SOME_VMEM = 48 * 2**20
VMEM = 60 * 2**20
NT = (((1,), (1,)), ((), ()))
NN = (((1,), (0,)), ((), ()))
TN = (((0,), (0,)), ((), ()))
F32 = jnp.float32
BF16 = jnp.bfloat16
SCALE = HEAD**-0.5
TILE = 256


def mm(a, b, dims):
    return lax.dot_general(a, b, dims, preferred_element_type=F32)


def col_sum(x):
    return jnp.sum(x, axis=0, keepdims=True)


def tile_at(i, tile=TILE):
    return pl.ds(pl.multiple_of(i * tile, tile), tile)


def parts(x):
    hi = x.astype(BF16)
    rest = x - hi.astype(F32)
    mid = rest.astype(BF16)
    return hi, mid, (rest - mid.astype(F32)).astype(BF16)


def same_half():
    a, b = (lax.broadcasted_iota(jnp.int32, (PAIR, PAIR), i) < HEAD for i in (0, 1))
    return jnp.where(a == b, 1.0, 0.0).astype(BF16)


def left_lanes():
    return lax.broadcasted_iota(jnp.int32, (1, PAIR), 1) < HEAD


def together(bands, whole):
    rows = bands[0].shape[0]
    for i, band in enumerate(bands):
        whole[i * rows:(i + 1) * rows, :] = band[...]


def attend_kernel(tiles, q_ref, k_own, k_mate, k_far, v_own, v_mate, v_far, qtag_ref, ktag_ref, o_ref, ext_ref,
                  kx, qx0, qx1, vt, acc0, acc1, top0, top1):
    rows, near = q_ref.shape[0], ktag_ref.shape[0]
    left = left_lanes()
    q_pair = q_ref[...] * jnp.asarray(SCALE, BF16)
    zero = jnp.zeros_like(q_pair)
    qx0[:, :PAIR] = jnp.where(left, q_pair, zero)
    qx1[:, :PAIR] = jnp.where(left, zero, q_pair)
    qx0[:, PAIR:] = qtag_ref[...]
    qx1[:, PAIR:] = qtag_ref[...]
    kx[:, PAIR:] = ktag_ref[...]
    vt[HEAD:PAIR, :] = jnp.ones((HEAD, near), BF16)
    halves = same_half()

    def longest(x):
        x = x.astype(F32)
        return jnp.max(mm((x * x).astype(BF16), halves, NN), axis=0, keepdims=True)

    reach = 0.0
    for i, (k_band, v_band) in enumerate(((k_own, v_own), (k_mate, v_mate), (k_far, v_far))):
        span = slice(i * rows, (i + 1) * rows)
        kx[span, :PAIR] = k_band[...]
        turned = v_band[...].T
        vt[:HEAD, span] = turned[:HEAD]
        vt[PAIR:, span] = turned[HEAD:]
        reach = jnp.maximum(reach, longest(k_band[...]))
    plain = jnp.max(reach * longest(q_pair)) < (SAFE * 0.98) ** 2
    heads = ((acc0, top0, qx0, slice(0, PAIR)), (acc1, top1, qx1, slice(HEAD, HEAD + PAIR)))
    for acc, *_ in heads:
        acc[...] = jnp.zeros_like(acc)

    @pl.when(plain)
    def _():
        for _, top, *_ in heads:
            top[...] = jnp.zeros_like(top)

        def per_band(band, _):
            for n in range(1, rows // TILE + 1):
                @pl.when(tiles[band] == n)
                def _():
                    ks = pl.ds(pl.multiple_of(band * rows, rows), n * TILE)
                    for acc, _, qx, at in heads:
                        p = jnp.exp(mm(kx[ks, :], qx[...], NT)).astype(BF16)
                        acc[...] += mm(vt[at, ks], p, NN)
            return 0

        lax.fori_loop(0, near // rows, per_band, 0)

    @pl.when(jnp.logical_not(plain))
    def _():
        for _, top, *_ in heads:
            top[...] = jnp.full_like(top, -3e38)

        def per_k(ki, _):
            @pl.when(lax.rem(ki, rows // TILE) < tiles[lax.div(ki, rows // TILE)])
            def _():
                ks = tile_at(ki)
                for acc, top, qx, at in heads:
                    s = mm(kx[ks, :], qx[...], NT)
                    old = top[...]
                    new = jnp.maximum(old, jnp.max(s, axis=0, keepdims=True))
                    p = jnp.exp(s - new[:1, :]).astype(BF16)
                    acc[...] = acc[...] * jnp.exp(old - new)[:1, :] + mm(vt[at, ks], p, NN)
                    top[...] = new
            return 0

        lax.fori_loop(0, near // TILE, per_k, 0)

    def finish(qi, _):
        qs = tile_at(qi)
        tags = qtag_ref[qs, :].astype(F32).T[:8]
        place = lax.broadcasted_iota(jnp.int32, (8, TILE), 0)
        out, ext = [], []
        for acc, top, _, at in heads:
            total, plain_out = (acc[HEAD:, qs], acc[:HEAD, qs]) if at.start == 0 else (acc[:HEAD, qs], acc[HEAD:, qs])
            out.append(plain_out / total)
            hi, mid, lo = (x.astype(F32) for x in parts(jnp.log(total[:8]) + top[:, qs]))
            head = jnp.where(place == 2, hi, jnp.where(place == 3, mid, jnp.where(place == 4, lo, tags)))
            ext += [head, jnp.zeros((HEAD - 8, TILE), F32)]
        o_ref[qs, :] = jnp.concatenate(out, axis=0).T.astype(BF16)
        ext_ref[qs, :] = jnp.concatenate(ext, axis=0).T.astype(BF16)
        return 0

    lax.fori_loop(0, rows // TILE, finish, 0)


def attend(q, k, v, qtag, ktag, tiles):
    rows, d = q.shape
    near = len(k) * rows
    part = lambda n: pl.BlockSpec((n, PAIR), lambda p, *_: (0, p))
    fixed = lambda n: pl.BlockSpec((n, PAIR), lambda p, *_: (0, 0))
    return pl.pallas_call(
        attend_kernel,
        grid_spec=pltpu.PrefetchScalarGridSpec(
            num_scalar_prefetch=1,
            grid=(d // PAIR,),
            in_specs=[part(rows)] + [part(rows)] * 6 + [fixed(rows), fixed(near)],
            out_specs=[part(rows)] * 2,
            scratch_shapes=[pltpu.VMEM((n, 2 * PAIR), BF16) for n in (near, rows, rows)] + [pltpu.VMEM((PAIR + HEAD, near), BF16)]
            + [pltpu.VMEM((PAIR, rows), F32)] * 2 + [pltpu.VMEM((8, rows), F32)] * 2,
        ),
        out_shape=[jax.ShapeDtypeStruct((rows, d), BF16)] * 2,
        compiler_params=pltpu.CompilerParams(vmem_limit_bytes=SOME_VMEM),
        cost_estimate=pl.CostEstimate(flops=40 * 10**9, bytes_accessed=16 * 2**20, transcendentals=0),
        name="attend",
    )(tiles, q, *k, *v, qtag, ktag)


def hull(qbits, want, nq):
    first, last = jnp.int32(nq), jnp.int32(0)
    for qi in reversed(range(nq)):
        hit = (qbits[qi] & want) != 0
        last = jnp.where(hit & (last == 0), qi + 1, last)
        first = jnp.where(hit, qi, first)
    return first, jnp.maximum(last - first, 0)


def attend_back_kernel(tk, qbits, kbits, q_ref, k_own, k_mate, k_far, v_own, v_mate, v_far, g_ref, o_ref, ext_ref, ktag_ref,
                       own_in, mate_in, far_in, sums_in, *refs):
    (sums, dq_ref, dk_ref, dv_ref, w_ref, k_ref, v_ref, qx0, qx1, gx0, gx1, qt, gt, dq_acc, dk_acc, dv_acc, own_ref, mate_ref,
     far_ref, arrived) = refs[-20:]
    rows, near = q_ref.shape[0], k_ref.shape[0]
    first = pl.program_id(0) == 0
    copies = [pltpu.make_async_copy(a, b, arrived.at[i])
              for i, (a, b) in enumerate(((own_in, own_ref), (mate_in, mate_ref), (far_in, far_ref)))]

    @pl.when(first)
    def _():
        for copy in copies:
            copy.start()

    together((k_own, k_mate, k_far), k_ref)
    together((v_own, v_mate, v_far), v_ref)
    nq = rows // TILE
    left = left_lanes()
    place = lax.broadcasted_iota(jnp.int32, (1, PAIR), 1) % HEAD
    halves = same_half()

    def per_q(qi, _):
        qs = tile_at(qi)
        q_pair, g_pair, ext = q_ref[qs, :], g_ref[qs, :], ext_ref[qs, :]
        qt[:, qs] = q_pair.T
        gt[:, qs] = g_pair.T
        zero = jnp.zeros_like(q_pair)
        hi, mid, _ = parts(g_pair.astype(F32) * o_ref[qs, :].astype(F32))
        hi, mid, _ = parts(mm(hi, halves, NN) + mm(mid, halves, NN))
        inner = jnp.where(place == 2, hi, jnp.where(place == 3, mid, zero))
        scaled = q_pair * jnp.asarray(SCALE, BF16)
        for x0, x1, base, more in ((qx0, qx1, scaled, ext), (gx0, gx1, g_pair, inner)):
            x0[qs, :PAIR] = jnp.where(left, base, zero)
            x1[qs, :PAIR] = jnp.where(left, zero, base)
            x0[qs, PAIR:] = jnp.where(left, more, zero)
            x1[qs, PAIR:] = jnp.where(left, zero, more)
        return 0

    lax.fori_loop(0, nq, per_q, 0)
    dq_acc[...] = jnp.zeros_like(dq_acc)

    def per_k(ki, _):
        first, count = hull(qbits, kbits[ki], nq)
        ks = tile_at(ki, tk)

        @pl.when(count == 0)
        def _():
            dk_acc[:, ks] = jnp.zeros((PAIR, tk), F32)
            dv_acc[:, ks] = jnp.zeros((PAIR, tk), F32)

        for n in range(1, nq + 1):
            @pl.when(count == n)
            def _():
                qs = pl.ds(pl.multiple_of(first * TILE, TILE), n * TILE)
                k_pair, tags = k_ref[ks, :], ktag_ref[ks, :]
                zero = jnp.zeros_like(k_pair)
                kx = jnp.concatenate([k_pair, tags], axis=1)
                vx = jnp.concatenate([v_ref[ks, :], tags], axis=1)
                dq = 0.0
                for qx, gx, at, kz in ((qx0, gx0, 0, jnp.where(left, k_pair, zero)),
                                       (qx1, gx1, HEAD, jnp.where(left, zero, k_pair))):
                    head = slice(at, at + HEAD)
                    p = jnp.exp(mm(qx[qs, :], kx, NT))
                    ds = (p * mm(gx[qs, :], vx, NT)).astype(BF16)
                    dv_acc[head, ks] = mm(gt[head, qs], p.astype(BF16), NN)
                    dk_acc[head, ks] = mm(qt[head, qs], ds, NN)
                    dq = dq + mm(ds, kz, NN)
                dq_acc[qs, :] += dq
        return 0

    lax.fori_loop(0, near // tk, per_k, 0)
    dq = (dq_acc[...] * SCALE).astype(BF16)
    dk = (dk_acc[...] * SCALE).astype(BF16)
    dv = dv_acc[...].astype(BF16)
    dq_ref[...] = dq
    dk_ref[...] = dk.T
    dv_ref[...] = dv.T

    @pl.when(first)
    def _():
        for copy in copies:
            copy.wait()

    w_ref[:, :PAIR] = mm(dq, own_ref[...], TN).T.astype(BF16)
    for i, x in ((1, dk), (2, dv)):
        total = mm(x[:, :rows], own_ref[...], NN)
        total = total + mm(x[:, rows:2 * rows], mate_ref[...], NN)
        total = total + mm(x[:, 2 * rows:], far_ref[...], NN)
        w_ref[:, i * PAIR:(i + 1) * PAIR] = total.T.astype(BF16)
    row = lax.broadcasted_iota(jnp.int32, (8, PAIR), 0)
    by_column = lambda ref: mm(jnp.ones((8, ref.shape[0]), BF16), ref[...], NN)
    sums[...] = jnp.where(row == 4, by_column(dq_ref), jnp.where(row == 5, by_column(dv_ref), sums_in[...]))


def attend_back(pair, pairs, kept, after, q, k, v, g, o, ext, ktag, inputs, qbits, kbits, tk):
    rows, d = q.shape
    near = len(k) * rows
    part = lambda n: pl.BlockSpec((n, PAIR), lambda p, *_: (0, pair + p))
    once = lambda n, m: pl.BlockSpec((n, m), lambda p, *_: (0, 0), pipeline_mode=pl.Buffered(1))
    sums = pl.BlockSpec((8, PAIR), lambda p, *_: (1, pair + p))
    hold = pl.BlockSpec(memory_space=pl.ANY)
    return pl.pallas_call(
        functools.partial(attend_back_kernel, tk),
        grid_spec=pltpu.PrefetchScalarGridSpec(
            num_scalar_prefetch=2,
            grid=(pairs,),
            in_specs=[part(rows)] * 10 + [once(near, PAIR)] + [hold] * 3 + [sums]
            + [hold] * (len(kept) - 1 + len(after)),
            out_specs=[sums, part(rows), part(near), part(near), pl.BlockSpec((d, 3 * PAIR), lambda p, *_: (0, p))],
            scratch_shapes=[pltpu.VMEM((near, PAIR), BF16)] * 2 + [pltpu.VMEM((rows, 2 * PAIR), BF16)] * 4
            + [pltpu.VMEM((PAIR, rows), BF16)] * 2 + [pltpu.VMEM((rows, PAIR), F32)] + [pltpu.VMEM((PAIR, near), F32)] * 2
            + [pltpu.VMEM((rows, d), BF16)] * 3 + [pltpu.SemaphoreType.DMA((3,))],
        ),
        out_shape=[jax.ShapeDtypeStruct((16, d), F32)] + [jax.ShapeDtypeStruct((n, d), BF16) for n in (rows, near, near)]
        + [jax.ShapeDtypeStruct((d, pairs * 3 * PAIR), BF16)],
        input_output_aliases={16 + i: i for i in range(len(kept))},
        compiler_params=pltpu.CompilerParams(vmem_limit_bytes=SOME_VMEM),
        cost_estimate=pl.CostEstimate(flops=18 * pairs * 10**9, bytes_accessed=8 * 2**20, transcendentals=0),
        name="attend_back",
    )(qbits, kbits, q, *k, *v, g, o, ext, ktag, *inputs, *kept, *after)


def project_kernel(x, w_key, w_value, b_value, *refs):
    k_ref, v_ref = refs[-2:]
    k_ref[...] = mm(x[...], w_key[...], NN).astype(BF16)
    v_ref[...] = (mm(x[...], w_value[...], NN) + b_value[...].reshape(1, -1)).astype(BF16)
    if len(refs) > 2:
        w_query, b_query, q_ref = refs[:3]
        q_ref[...] = (mm(x[...], w_query[...], NN) + b_query[...].reshape(1, -1)).astype(BF16)


def project(x, w_key, w_value, b_value, *query):
    rows, d = x.shape
    tr = rows // 2
    tile = pl.BlockSpec((tr, d), lambda i: (i, 0))
    whole = pl.BlockSpec((d, d), lambda i: (0, 0), pipeline_mode=pl.Buffered(1))
    flat = pl.BlockSpec((d,), lambda i: (0,))
    outs = 3 if query else 2
    return pl.pallas_call(
        project_kernel,
        grid=(rows // tr,),
        in_specs=[tile, whole, whole, flat] + [whole, flat] * (outs - 2),
        out_specs=[tile] * outs,
        out_shape=[jax.ShapeDtypeStruct((rows, d), BF16)] * outs,
        compiler_params=pltpu.CompilerParams(vmem_limit_bytes=VMEM),
        cost_estimate=pl.CostEstimate(flops=6 * rows * d * d, bytes_accessed=10 * rows * d, transcendentals=0),
        name="project",
    )(x, w_key, w_value, b_value, *query)


def row_norm(values):
    centred = values - jnp.mean(values, axis=-1, keepdims=True)
    rstd = lax.rsqrt(jnp.mean(centred * centred, axis=-1, keepdims=True) + 1e-12)
    return centred * rstd, rstd


def norm_back(cot, gain, normed, rstd):
    e = cot * gain
    return rstd * (e - jnp.mean(e, axis=-1, keepdims=True) - normed * jnp.mean(e * normed, axis=-1, keepdims=True))


def dense_kernel(tf, hidden, mixed, out_grad, mask, w_out, up_in, down_in, b_out, gain_one, shift_one, b_up, b_down,
                 gain_two, shift_two, result, low_out, active, d_branch, d_upper, d_one, d_att, d_mixed, sums, slope,
                 sum_up, w_up, w_down, arrived):
    ff = w_up.shape[1]
    start = pl.program_id(0) == 0
    copies = [pltpu.make_async_copy(a, b, arrived.at[i]) for i, (a, b) in enumerate(((up_in, w_up), (down_in, w_down)))]

    @pl.when(start)
    def _():
        for copy in copies:
            copy.start()
        sums[...] = jnp.zeros_like(sums)
        sum_up[...] = jnp.zeros_like(sum_up)

    vec = lambda ref: ref[...].reshape(1, -1)
    r1 = hidden[...].astype(F32) + (mm(mixed[...], w_out[...], NN) + vec(b_out))
    n1, s1 = row_norm(r1)
    normed_one = n1 * vec(gain_one) + vec(shift_one)
    low = normed_one.astype(BF16)
    low_out[...] = low
    branch = jnp.zeros_like(r1)
    bias = vec(b_up)

    @pl.when(start)
    def _():
        for copy in copies:
            copy.wait()

    for t in range(0, ff, tf):
        c = pl.ds(t, tf)
        u = mm(low, w_up[:, c], NN) + bias[:, t:t + tf]
        phi = 0.5 + 0.5 * lax.erf(u * (0.5**0.5))
        a = (u * phi).astype(BF16)
        active[:, c] = a
        slope[:, c] = phi + u * (jnp.exp(u * u * -0.5) * 0.3989422804014327)
        branch = branch + mm(a, w_down[c, :], NN)
    n2, s2 = row_norm(normed_one + (branch + vec(b_down)))
    result[...] = (n2 * vec(gain_two) + vec(shift_two)).astype(BF16)
    cot = out_grad[...].astype(F32) * mask[...]
    d_two = norm_back(cot, vec(gain_two), n2, s2)
    db = d_two.astype(BF16)
    d_branch[...] = db
    sums[0:1, :] += col_sum(cot * n2)
    sums[1:2, :] += col_sum(cot)
    sums[2:3, :] += col_sum(db.astype(F32))
    d_normed = d_two
    for t in range(0, ff, tf):
        c = pl.ds(t, tf)
        du = (mm(db, w_down[c, :], NT) * slope[:, c]).astype(BF16)
        d_upper[:, c] = du
        sum_up[:, c] += col_sum(du.astype(F32))
        d_normed = d_normed + mm(du, w_up[:, c], NT)
    sums[3:4, :] += col_sum(d_normed * n1)
    sums[4:5, :] += col_sum(d_normed)
    d1 = norm_back(d_normed, vec(gain_one), n1, s1)
    d_one[...] = d1
    da = d1.astype(BF16)
    d_att[...] = da
    sums[5:6, :] += col_sum(da.astype(F32))
    d_mixed[...] = mm(da, w_out[...], NT).astype(BF16)

    @pl.when(pl.program_id(0) == pl.num_programs(0) - 1)
    def _():
        d = hidden.shape[1]
        for i in range(ff // d):
            sums[8 + i:9 + i, :] = sum_up[:, i * d:(i + 1) * d]


def dense(hidden, mixed, out_grad, mask, w_out, w_up, w_down, b_out, gain_one, shift_one, b_up, b_down, gain_two,
          shift_two, tr=256, tf=768):
    rows, d = hidden.shape
    ff = w_up.shape[1]
    row = lambda n: pl.BlockSpec((tr, n), lambda i: (i, 0))
    whole = lambda a, b: pl.BlockSpec((a, b), lambda i: (0, 0), pipeline_mode=pl.Buffered(1))
    flat = lambda n: pl.BlockSpec((n,), lambda i: (0,))
    shape = jax.ShapeDtypeStruct
    low = shape((rows, d), BF16)
    return pl.pallas_call(
        functools.partial(dense_kernel, tf),
        grid=(rows // tr,),
        in_specs=[row(d), row(d), row(d), row(1), whole(d, d)] + [pl.BlockSpec(memory_space=pl.ANY)] * 2 + [flat(d), flat(d), flat(d),
                  flat(ff), flat(d), flat(d), flat(d)],
        out_specs=[row(d), row(d), row(ff), row(d), row(ff), row(d), row(d), row(d),
                   pl.BlockSpec((16, d), lambda i: (0, 0))],
        out_shape=[low, low, shape((rows, ff), BF16), low, shape((rows, ff), BF16), shape((rows, d), F32), low, low,
                   shape((16, d), F32)],
        scratch_shapes=[pltpu.VMEM((tr, ff), F32), pltpu.VMEM((1, ff), F32), pltpu.VMEM((d, ff), BF16), pltpu.VMEM((ff, d), BF16),
                        pltpu.SemaphoreType.DMA((2,))],
        compiler_params=pltpu.CompilerParams(vmem_limit_bytes=VMEM),
        cost_estimate=pl.CostEstimate(flops=40 * 10**9, bytes_accessed=40 * 2**20, transcendentals=0),
        name="dense",
    )(hidden, mixed, out_grad, mask.astype(F32).reshape(-1, 1), w_out, w_up, w_down, b_out, gain_one, shift_one, b_up,
      b_down, gain_two, shift_two)


def back_kernel(dk, dv, w_key, w_value, *refs):
    total = mm(dk[...], w_key[...], NT) + mm(dv[...], w_value[...], NT)
    if len(refs) > 1:
        dq, w_query, d_one, mate_part, far_part = refs[:5]
        total = total + mm(dq[...], w_query[...], NT) + d_one[...]
        total = total + mate_part[...].astype(F32) + far_part[...].astype(F32)
    refs[-1][...] = total.astype(BF16)


def back_product(band, dk, dv, w_key, w_value, own=()):
    d = w_key.shape[0]
    rows = dk.shape[0] // 3
    tr = rows // 2
    at = lambda i: (band * (rows // tr) + i, 0)
    row = lambda place: pl.BlockSpec((tr, d), place)
    whole = pl.BlockSpec((d, d), lambda i: (0, 0), pipeline_mode=pl.Buffered(1))
    first = lambda i: (i, 0)
    return pl.pallas_call(
        back_kernel,
        grid=(rows // tr,),
        in_specs=[row(at), row(at), whole, whole] + ([row(first), whole] + [row(first)] * 3 if own else []),
        out_specs=row(first),
        out_shape=jax.ShapeDtypeStruct((rows, d), BF16),
        compiler_params=pltpu.CompilerParams(vmem_limit_bytes=VMEM),
        cost_estimate=pl.CostEstimate(flops=(6 if own else 4) * rows * d * d, bytes_accessed=10 * rows * d, transcendentals=0),
        name="back_product",
    )(dk, dv, w_key, w_value, *own)


ALL = ("page", "band")


def everyone():
    return lax.axis_size("page") * lax.axis_size("band")


def swapped(block, mask):
    return lax.ppermute(block, ALL, [(i, i ^ mask) for i in range(everyone())])


def side(bit):
    return lax.rem(lax.div(lax.axis_index(ALL), bit), 2)


def masks_of(bits):
    masks = [0]
    for bit in reversed(bits):
        masks = masks + [mask | bit for mask in masks]
    return masks


def place_of(bits):
    at = 0
    for bit in bits:
        at = 2 * at + side(bit)
    return at


def dealt(block, bits, axis):
    masks = masks_of(bits)
    size = block.shape[axis] // len(masks)
    place = place_of(bits)
    return [lax.dynamic_slice_in_dim(block, jnp.bitwise_xor(place, i) * size, size, axis) for i in range(len(masks))]


def sent(parts, bits):
    return [swapped(part, mask) for part, mask in zip(parts, masks_of(bits)[1:])]


def summed(parts):
    parts = [part.astype(F32) for part in parts]
    while len(parts) > 1:
        parts = [parts[i] + parts[i + 1] for i in range(0, len(parts), 2)]
    return parts[0].astype(BF16)


class Summing:
    def __init__(self, parts, stages):
        self.stages, self.at = stages, 0
        self.parts = parts

    def advance(self, held=None):
        if self.at < len(self.stages):
            theirs = sent(self.parts[1:], self.stages[self.at])
            if held is not None:
                theirs, held = lax.optimization_barrier((theirs, held))
            block = summed([self.parts[0]] + theirs)
            self.at += 1
            self.parts = dealt(block, self.stages[self.at], 0) if self.at < len(self.stages) else [block]
        return held


def in_order(parts, bits):
    for i, bit in enumerate(bits):
        far = 1 << (len(bits) - 1 - i)
        flip = side(bit) == 1
        parts = [jnp.where(flip, parts[j ^ far], parts[j]) for j in range(len(parts))]
    return jnp.concatenate(parts)


def products_kernel(low, mixed, d_branch, d_upper, d_att, active, made, turned):
    step = pl.program_id(0)
    count = (pl.num_programs(0) - 1) // 2
    for at, left in ((0, low), (count, mixed), (count + 1, d_branch)):
        @pl.when(step == at)
        def _():
            turned[...] = left[...].T

    for here, right in ((step < count, d_upper), (step == count, d_att), (step > count, active)):
        @pl.when(here)
        def _():
            made[...] = mm(turned[...], right[...], NN).astype(BF16)


def feed_forward_products(low, mixed, d_branch, d_upper, d_att, active):
    rows, d = low.shape
    count = active.shape[1] // d
    once = pl.BlockSpec((rows, d), lambda j: (0, 0), pipeline_mode=pl.Buffered(1))
    along = lambda first: pl.BlockSpec((rows, d), lambda j: (0, jnp.clip(j - first, 0, count - 1)))
    return pl.pallas_call(
        products_kernel,
        grid=(2 * count + 1,),
        in_specs=[once, once, once, along(0), once, along(count + 1)],
        out_specs=pl.BlockSpec((d, d), lambda j: (0, j)),
        out_shape=jax.ShapeDtypeStruct((d, (2 * count + 1) * d), BF16),
        scratch_shapes=[pltpu.VMEM((d, rows), BF16)],
        compiler_params=pltpu.CompilerParams(vmem_limit_bytes=VMEM),
        cost_estimate=pl.CostEstimate(flops=2 * rows * d * d * (2 * count + 1), bytes_accessed=20 * d * d * count,
                                      transcendentals=0),
        name="products",
    )(low, mixed, d_branch, d_upper, d_att, active)


def place_kernel(got, down, up, out):
    d = out.shape[1]
    ff = up.shape[1]
    up[...] = got[:, :ff].astype(F32)
    out[...] = got[:, ff:ff + d].astype(F32)
    for c in range(0, ff, d):
        down[c:c + d, :] = got[:, ff + d + c:ff + 2 * d + c].astype(F32).T


def feed_forward_whole(got):
    d = got.shape[0]
    ff = (got.shape[1] - d) // 2
    row = lambda n: pl.BlockSpec((PAIR, n), lambda j: (j, 0))
    return pl.pallas_call(
        place_kernel,
        grid=(d // PAIR,),
        in_specs=[row(2 * ff + d)],
        out_specs=[pl.BlockSpec((ff, PAIR), lambda j: (0, j)), row(ff), row(d)],
        out_shape=[jax.ShapeDtypeStruct(shape, F32) for shape in ((ff, d), (d, ff), (d, d))],
        compiler_params=pltpu.CompilerParams(vmem_limit_bytes=VMEM),
        cost_estimate=pl.CostEstimate(flops=0, bytes_accessed=12 * ff * d, transcendentals=0),
        name="place",
    )(got)


def split_kernel(x, q, k, v):
    for i, out in enumerate((q, k, v)):
        for p in range(q.shape[1] // PAIR):
            at = (3 * p + i) * PAIR
            out[:, p * PAIR:(p + 1) * PAIR] = x[:, at:at + PAIR].astype(F32)


def split_projections(x):
    d = x.shape[0]
    tr = d // 3
    row = lambda n: pl.BlockSpec((tr, n), lambda i: (i, 0))
    return pl.pallas_call(
        split_kernel,
        grid=(3,),
        in_specs=[row(3 * d)],
        out_specs=[row(d)] * 3,
        out_shape=[jax.ShapeDtypeStruct((d, d), F32)] * 3,
        compiler_params=pltpu.CompilerParams(vmem_limit_bytes=32 * 2**20),
        cost_estimate=pl.CostEstimate(flops=0, bytes_accessed=18 * d * d, transcendentals=0),
        name="split",
    )(x)


def tag_columns(page_ids, near_tags):
    place = jnp.arange(PAIR)[None, :] % HEAD
    qtag = jnp.where(jnp.arange(PAIR)[None, :] == page_ids[:, None], 1.0, 0.0).astype(BF16)
    ktag = jnp.where((place < 2) & (near_tags[:, None] != place + 1), BLOCKED, 0.0)
    return qtag, jnp.where((place >= 2) & (place < 5), -1.0, ktag).astype(BF16)


def tokens_of(near_tags, rows):
    have = jnp.sum((near_tags.reshape(-1, rows) > 0).astype(jnp.int32), axis=1)
    return (have + (TILE - 1)) // TILE


def tile_bits(tags, tile):
    tags = tags.reshape(-1, tile)
    return sum(jnp.max(jnp.where(tags == d + 1, 1 << d, 0), axis=1) for d in range(2)).astype(jnp.int32)


def body(hidden, page_ids, key_mask, out_grad, w_query, b_query, w_key, w_value, b_value, w_out, b_out, gain_one,
         shift_one, w_up, b_up, w_down, b_down, gain_two, shift_two):
    rows, d = hidden.shape
    bands = lax.axis_size("band")
    mates = [(i, i ^ 1) for i in range(bands)]
    across = [(i, i + 1) for i in range(1, bands - 1, 2)] + [(i + 1, i) for i in range(1, bands - 1, 2)]
    to_mate = lambda x: lax.ppermute(x, "band", mates)
    to_across = lambda x: lax.ppermute(x, "band", across)

    key_tags = jnp.where(key_mask == 1, page_ids + 1, 0)
    far, mate = to_across(hidden), to_mate(hidden)
    near_tags = jnp.concatenate([key_tags, to_mate(key_tags), to_across(key_tags)])
    queries, *own_pair = project(hidden, w_key, w_value, b_value, w_query, b_query)
    mate_pair, far_pair = project(mate, w_key, w_value, b_value), project(far, w_key, w_value, b_value)
    keys, values = zip(own_pair, mate_pair, far_pair)
    qtag, ktag = tag_columns(page_ids, near_tags)
    tk = 512
    tokens, qbits, kbits = tokens_of(near_tags, rows), tile_bits(key_tags, TILE), tile_bits(near_tags, tk)
    tokens, qbits, kbits, queries = lax.optimization_barrier((tokens, qbits, kbits, queries))

    mixed, ext = attend(queries, keys, values, qtag, ktag, tokens)
    (result, normed_low, active, d_branch, d_upper, d_one, d_att, d_mixed, sums) = dense(
        hidden, mixed, out_grad, key_mask, w_out, w_up, w_down, b_out, gain_one, shift_one, b_up, b_down, gain_two,
        shift_two)

    count = everyone().bit_length() - 1
    core, y, x, z = 1, 2, bands, 2 * bands
    rest = [1 << i for i in range(count) if 1 << i not in (core, y, x, z)]
    direct = [[core], [x, y]] + [([z] + rest)[i:i + 2] for i in range(0, 1 + len(rest), 2)]

    products = feed_forward_products(normed_low, mixed, d_branch, d_upper, d_att, active)
    products, d_mixed = lax.optimization_barrier((products, d_mixed))
    shares = lax.psum_scatter(products, ALL, scatter_dimension=0, tiled=True)

    pairs = d // PAIR
    kept, made, at, after = (sums,), [], 0, []
    for size in (2, 2, pairs - 4):
        *kept, made_now = attend_back(at, size, kept, after, queries, keys, values, d_mixed, mixed, ext, ktag,
                                      (hidden, mate, far), qbits, kbits, tk)
        at += size
        made.append(made_now)
        if at == 2:
            early = Summing(dealt(made[0], [core], 0), direct[:2])
            after = early.parts
        elif at == 4:
            kept[1] = early.advance(kept[1])
            late = Summing(dealt(made[1], [core], 0), direct[:1])
            after = early.parts + late.parts
    for stream in (early, late):
        kept[1] = stream.advance(kept[1])
    vectors, dq, dk, dv = kept

    keep, send = dealt(made[-1], [core], 0)
    vectors = vectors.astype(BF16)
    dk, send = lax.optimization_barrier((dk, send))
    theirs = [swapped(send, core), swapped(vectors, core)]
    far_part = back_product(2, dk, dv, w_key, w_value)
    theirs, far_part = lax.optimization_barrier((theirs, far_part))
    block = jnp.concatenate([late.parts[0], summed([keep, theirs[0]])], axis=1)
    vectors = summed([vectors, theirs[1]])
    vectors = jnp.concatenate([vectors[:8], vectors[8:]], axis=1)
    for i, bits in enumerate(direct[1:]):
        parts = dealt(block, bits, 0)
        send = [jnp.concatenate([part, vectors]) for part in parts[1:]]
        if i == 0:
            send, dk = lax.optimization_barrier((send, dk))
            theirs = sent(send, bits)
            mate_part = back_product(1, dk, dv, w_key, w_value)
            theirs, mate_part, shares = lax.optimization_barrier((theirs, mate_part, shares))
            got = lax.all_gather(shares, ALL, axis=0, tiled=True)
        else:
            theirs = sent(send, bits)
        size = parts[0].shape[0]
        block = summed([parts[0]] + [other[:size] for other in theirs])
        vectors = summed([vectors] + [other[size:] for other in theirs])
        if i == 0:
            block = jnp.concatenate([early.parts[0], block], axis=1)
            vectors = jnp.pad(vectors, ((0, 0), (0, block.shape[1] - vectors.shape[1])))
            block, far_part, mate_part = lax.optimization_barrier((block, far_part, mate_part))
            far_part, mate_part = to_across(far_part), to_mate(mate_part)
    vectors = jnp.concatenate([vectors[:, :d], vectors[:, d:2 * d]]).astype(F32)

    for i, bits in enumerate(reversed(direct)):
        theirs = sent([block] * (len(masks_of(bits)) - 1), bits)
        if i == len(direct) - 3:
            input_grad = back_product(0, dk, dv, w_key, w_value, (dq, w_query, d_one, mate_part, far_part))
            theirs, input_grad = lax.optimization_barrier((theirs, input_grad))
        block = in_order([block] + theirs, bits)
    grad_query, grad_key, grad_value = split_projections(block)
    got, grad_query = lax.optimization_barrier((got, grad_query))
    grad_down, grad_up, grad_out = feed_forward_whole(got)
    return (
        result,
        input_grad,
        grad_query,
        vectors[12],
        grad_key,
        grad_value,
        vectors[13],
        grad_out,
        vectors[5],
        vectors[3],
        vectors[4],
        grad_up,
        vectors[8:12].reshape(-1),
        grad_down,
        vectors[2],
        vectors[0],
        vectors[1],
    )


def solution(mesh):
    split = P(("page", "band"), None)
    line = P(("page", "band"))
    return jax.shard_map(
        body,
        mesh=mesh,
        in_specs=(split, line, line, split) + (P(),) * 15,
        out_specs=(split, split) + (P(),) * 15,
        check_vma=False,
    )
```

```python
import functools

import jax
import jax.numpy as jnp
from jax import lax
from jax.experimental import pallas as pl
from jax.experimental.pallas import tpu as pltpu
from jax.sharding import PartitionSpec as P


HEAD = 64
PAIR = 128
BLOCKED = -1e30
SAFE = 60.0
SOME_VMEM = 48 * 2**20
VMEM = 60 * 2**20
NT = (((1,), (1,)), ((), ()))
NN = (((1,), (0,)), ((), ()))
TN = (((0,), (0,)), ((), ()))
F32 = jnp.float32
BF16 = jnp.bfloat16
SCALE = HEAD**-0.5
TILE = 256


def mm(a, b, dims):
    return lax.dot_general(a, b, dims, preferred_element_type=F32)


def col_sum(x):
    return jnp.sum(x, axis=0, keepdims=True)


def tile_at(i, tile=TILE):
    return pl.ds(pl.multiple_of(i * tile, tile), tile)


def parts(x):
    hi = x.astype(BF16)
    rest = x - hi.astype(F32)
    mid = rest.astype(BF16)
    return hi, mid, (rest - mid.astype(F32)).astype(BF16)


def same_half():
    a, b = (lax.broadcasted_iota(jnp.int32, (PAIR, PAIR), i) < HEAD for i in (0, 1))
    return jnp.where(a == b, 1.0, 0.0).astype(BF16)


def left_lanes():
    return lax.broadcasted_iota(jnp.int32, (1, PAIR), 1) < HEAD


def together(bands, whole):
    rows = bands[0].shape[0]
    for i, band in enumerate(bands):
        whole[i * rows:(i + 1) * rows, :] = band[...]


def attend_kernel(tiles, q_ref, k_own, k_mate, k_far, v_own, v_mate, v_far, qtag_ref, ktag_ref, o_ref, ext_ref,
                  kx, qx0, qx1, vt, acc0, acc1, top0, top1):
    rows, near = q_ref.shape[0], ktag_ref.shape[0]
    left = left_lanes()
    q_pair = q_ref[...] * jnp.asarray(SCALE, BF16)
    zero = jnp.zeros_like(q_pair)
    qx0[:, :PAIR] = jnp.where(left, q_pair, zero)
    qx1[:, :PAIR] = jnp.where(left, zero, q_pair)
    qx0[:, PAIR:] = qtag_ref[...]
    qx1[:, PAIR:] = qtag_ref[...]
    kx[:, PAIR:] = ktag_ref[...]
    vt[HEAD:PAIR, :] = jnp.ones((HEAD, near), BF16)
    halves = same_half()

    def longest(x):
        x = x.astype(F32)
        return jnp.max(mm((x * x).astype(BF16), halves, NN), axis=0, keepdims=True)

    reach = 0.0
    for i, (k_band, v_band) in enumerate(((k_own, v_own), (k_mate, v_mate), (k_far, v_far))):
        span = slice(i * rows, (i + 1) * rows)
        kx[span, :PAIR] = k_band[...]
        turned = v_band[...].T
        vt[:HEAD, span] = turned[:HEAD]
        vt[PAIR:, span] = turned[HEAD:]
        reach = jnp.maximum(reach, longest(k_band[...]))
    plain = jnp.max(reach * longest(q_pair)) < (SAFE * 0.98) ** 2
    heads = ((acc0, top0, qx0, slice(0, PAIR)), (acc1, top1, qx1, slice(HEAD, HEAD + PAIR)))
    for acc, *_ in heads:
        acc[...] = jnp.zeros_like(acc)

    @pl.when(plain)
    def _():
        for _, top, *_ in heads:
            top[...] = jnp.zeros_like(top)

        def per_band(band, _):
            for n in range(1, rows // TILE + 1):
                @pl.when(tiles[band] == n)
                def _():
                    ks = pl.ds(pl.multiple_of(band * rows, rows), n * TILE)
                    scores = [mm(kx[ks, :], qx[...], NT) for _, _, qx, _ in heads]
                    probs = [jnp.exp(s).astype(BF16) for s in scores]
                    for (acc, _, _, at), p in zip(heads, probs):
                        acc[...] += mm(vt[at, ks], p, NN)
            return 0

        lax.fori_loop(0, near // rows, per_band, 0)

    @pl.when(jnp.logical_not(plain))
    def _():
        for _, top, *_ in heads:
            top[...] = jnp.full_like(top, -3e38)

        def per_k(ki, _):
            @pl.when(lax.rem(ki, rows // TILE) < tiles[lax.div(ki, rows // TILE)])
            def _():
                ks = tile_at(ki)
                for acc, top, qx, at in heads:
                    s = mm(kx[ks, :], qx[...], NT)
                    old = top[...]
                    new = jnp.maximum(old, jnp.max(s, axis=0, keepdims=True))
                    p = jnp.exp(s - new[:1, :]).astype(BF16)
                    acc[...] = acc[...] * jnp.exp(old - new)[:1, :] + mm(vt[at, ks], p, NN)
                    top[...] = new
            return 0

        lax.fori_loop(0, near // TILE, per_k, 0)

    def finish(qi, _):
        qs = tile_at(qi)
        tags = qtag_ref[qs, :].astype(F32).T[:8]
        place = lax.broadcasted_iota(jnp.int32, (8, TILE), 0)
        out, ext = [], []
        for acc, top, _, at in heads:
            total, plain_out = (acc[HEAD:, qs], acc[:HEAD, qs]) if at.start == 0 else (acc[:HEAD, qs], acc[HEAD:, qs])
            out.append(plain_out / total)
            hi, mid, lo = (x.astype(F32) for x in parts(jnp.log(total[:8]) + top[:, qs]))
            head = jnp.where(place == 2, hi, jnp.where(place == 3, mid, jnp.where(place == 4, lo, tags)))
            ext += [head, jnp.zeros((HEAD - 8, TILE), F32)]
        o_ref[qs, :] = jnp.concatenate(out, axis=0).T.astype(BF16)
        ext_ref[qs, :] = jnp.concatenate(ext, axis=0).T.astype(BF16)
        return 0

    lax.fori_loop(0, rows // TILE, finish, 0)


def attend(q, k, v, qtag, ktag, tiles):
    rows, d = q.shape
    near = len(k) * rows
    part = lambda n: pl.BlockSpec((n, PAIR), lambda p, *_: (0, p))
    fixed = lambda n: pl.BlockSpec((n, PAIR), lambda p, *_: (0, 0))
    return pl.pallas_call(
        attend_kernel,
        grid_spec=pltpu.PrefetchScalarGridSpec(
            num_scalar_prefetch=1,
            grid=(d // PAIR,),
            in_specs=[part(rows)] + [part(rows)] * 6 + [fixed(rows), fixed(near)],
            out_specs=[part(rows)] * 2,
            scratch_shapes=[pltpu.VMEM((n, 2 * PAIR), BF16) for n in (near, rows, rows)] + [pltpu.VMEM((PAIR + HEAD, near), BF16)]
            + [pltpu.VMEM((PAIR, rows), F32)] * 2 + [pltpu.VMEM((8, rows), F32)] * 2,
        ),
        out_shape=[jax.ShapeDtypeStruct((rows, d), BF16)] * 2,
        compiler_params=pltpu.CompilerParams(vmem_limit_bytes=VMEM),
        cost_estimate=pl.CostEstimate(flops=40 * 10**9, bytes_accessed=16 * 2**20, transcendentals=0),
        name="attend",
    )(tiles, q, *k, *v, qtag, ktag)


def hull(qbits, want, nq):
    first, last = jnp.int32(nq), jnp.int32(0)
    for qi in reversed(range(nq)):
        hit = (qbits[qi] & want) != 0
        last = jnp.where(hit & (last == 0), qi + 1, last)
        first = jnp.where(hit, qi, first)
    return first, jnp.maximum(last - first, 0)


def attend_back_kernel(tk, qbits, kbits, q_ref, k_own, k_mate, k_far, v_own, v_mate, v_far, g_ref, o_ref, ext_ref, ktag_ref,
                       own_in, mate_in, far_in, sums_in, *refs):
    (sums, dq_ref, dk_ref, dv_ref, w_ref, k_ref, v_ref, qx0, qx1, gx0, gx1, qt, gt, dq_acc, dk_acc, dv_acc, own_ref, mate_ref,
     far_ref, arrived) = refs[-20:]
    rows, near = q_ref.shape[0], k_ref.shape[0]
    first = pl.program_id(0) == 0
    copies = [pltpu.make_async_copy(a, b, arrived.at[i])
              for i, (a, b) in enumerate(((own_in, own_ref), (mate_in, mate_ref), (far_in, far_ref)))]

    @pl.when(first)
    def _():
        for copy in copies:
            copy.start()

    together((k_own, k_mate, k_far), k_ref)
    together((v_own, v_mate, v_far), v_ref)
    nq = rows // TILE
    left = left_lanes()
    place = lax.broadcasted_iota(jnp.int32, (1, PAIR), 1) % HEAD
    halves = same_half()

    def per_q(qi, _):
        qs = tile_at(qi)
        q_pair, g_pair, ext = q_ref[qs, :], g_ref[qs, :], ext_ref[qs, :]
        qt[:, qs] = q_pair.T
        gt[:, qs] = g_pair.T
        zero = jnp.zeros_like(q_pair)
        hi, mid, _ = parts(g_pair.astype(F32) * o_ref[qs, :].astype(F32))
        hi, mid, _ = parts(mm(hi, halves, NN) + mm(mid, halves, NN))
        inner = jnp.where(place == 2, hi, jnp.where(place == 3, mid, zero))
        scaled = q_pair * jnp.asarray(SCALE, BF16)
        for x0, x1, base, more in ((qx0, qx1, scaled, ext), (gx0, gx1, g_pair, inner)):
            x0[qs, :PAIR] = jnp.where(left, base, zero)
            x1[qs, :PAIR] = jnp.where(left, zero, base)
            x0[qs, PAIR:] = jnp.where(left, more, zero)
            x1[qs, PAIR:] = jnp.where(left, zero, more)
        return 0

    lax.fori_loop(0, nq, per_q, 0)
    dq_acc[...] = jnp.zeros_like(dq_acc)

    def per_k(ki, _):
        first, count = hull(qbits, kbits[ki], nq)
        ks = tile_at(ki, tk)

        @pl.when(count == 0)
        def _():
            dk_acc[:, ks] = jnp.zeros((PAIR, tk), F32)
            dv_acc[:, ks] = jnp.zeros((PAIR, tk), F32)

        for n in range(1, nq + 1):
            @pl.when(count == n)
            def _():
                qs = pl.ds(pl.multiple_of(first * TILE, TILE), n * TILE)
                k_pair, tags = k_ref[ks, :], ktag_ref[ks, :]
                zero = jnp.zeros_like(k_pair)
                kx = jnp.concatenate([k_pair, tags], axis=1)
                vx = jnp.concatenate([v_ref[ks, :], tags], axis=1)
                s0 = mm(qx0[qs, :], kx, NT)
                d0 = mm(gx0[qs, :], vx, NT)
                p0 = jnp.exp(s0)
                s1 = mm(qx1[qs, :], kx, NT)
                ds0 = (p0 * d0).astype(BF16)
                p0 = p0.astype(BF16)
                d1 = mm(gx1[qs, :], vx, NT)
                p1 = jnp.exp(s1)
                dv_acc[:HEAD, ks] = mm(gt[:HEAD, qs], p0, NN)
                dk_acc[:HEAD, ks] = mm(qt[:HEAD, qs], ds0, NN)
                ds1 = (p1 * d1).astype(BF16)
                p1 = p1.astype(BF16)
                dq = mm(ds0, jnp.where(left, k_pair, zero), NN)
                dv_acc[HEAD:, ks] = mm(gt[HEAD:, qs], p1, NN)
                dk_acc[HEAD:, ks] = mm(qt[HEAD:, qs], ds1, NN)
                dq = dq + mm(ds1, jnp.where(left, zero, k_pair), NN)
                dq_acc[qs, :] += dq
        return 0

    lax.fori_loop(0, near // tk, per_k, 0)
    dq = (dq_acc[...] * SCALE).astype(BF16)
    dk = (dk_acc[...] * SCALE).astype(BF16)
    dv = dv_acc[...].astype(BF16)
    dq_ref[...] = dq
    dk_ref[...] = dk.T
    dv_ref[...] = dv.T

    @pl.when(first)
    def _():
        for copy in copies:
            copy.wait()

    w_ref[:, :PAIR] = mm(dq, own_ref[...], TN).T.astype(BF16)
    for i, x in ((1, dk), (2, dv)):
        total = mm(x[:, :rows], own_ref[...], NN)
        total = total + mm(x[:, rows:2 * rows], mate_ref[...], NN)
        total = total + mm(x[:, 2 * rows:], far_ref[...], NN)
        w_ref[:, i * PAIR:(i + 1) * PAIR] = total.T.astype(BF16)
    row = lax.broadcasted_iota(jnp.int32, (8, PAIR), 0)
    by_column = lambda ref: mm(jnp.ones((8, ref.shape[0]), BF16), ref[...], NN)
    sums[...] = jnp.where(row == 4, by_column(dq_ref), jnp.where(row == 5, by_column(dv_ref), sums_in[...]))


def attend_back(pair, pairs, kept, after, q, k, v, g, o, ext, ktag, inputs, qbits, kbits, tk):
    rows, d = q.shape
    near = len(k) * rows
    part = lambda n: pl.BlockSpec((n, PAIR), lambda p, *_: (0, pair + p))
    once = lambda n, m: pl.BlockSpec((n, m), lambda p, *_: (0, 0), pipeline_mode=pl.Buffered(1))
    sums = pl.BlockSpec((8, PAIR), lambda p, *_: (1, pair + p))
    hold = pl.BlockSpec(memory_space=pl.ANY)
    return pl.pallas_call(
        functools.partial(attend_back_kernel, tk),
        grid_spec=pltpu.PrefetchScalarGridSpec(
            num_scalar_prefetch=2,
            grid=(pairs,),
            in_specs=[part(rows)] * 10 + [once(near, PAIR)] + [hold] * 3 + [sums]
            + [hold] * (len(kept) - 1 + len(after)),
            out_specs=[sums, part(rows), part(near), part(near), pl.BlockSpec((d, 3 * PAIR), lambda p, *_: (0, p))],
            scratch_shapes=[pltpu.VMEM((near, PAIR), BF16)] * 2 + [pltpu.VMEM((rows, 2 * PAIR), BF16)] * 4
            + [pltpu.VMEM((PAIR, rows), BF16)] * 2 + [pltpu.VMEM((rows, PAIR), F32)] + [pltpu.VMEM((PAIR, near), F32)] * 2
            + [pltpu.VMEM((rows, d), BF16)] * 3 + [pltpu.SemaphoreType.DMA((3,))],
        ),
        out_shape=[jax.ShapeDtypeStruct((16, d), F32)] + [jax.ShapeDtypeStruct((n, d), BF16) for n in (rows, near, near)]
        + [jax.ShapeDtypeStruct((d, pairs * 3 * PAIR), BF16)],
        input_output_aliases={16 + i: i for i in range(len(kept))},
        compiler_params=pltpu.CompilerParams(vmem_limit_bytes=SOME_VMEM),
        cost_estimate=pl.CostEstimate(flops=18 * pairs * 10**9, bytes_accessed=8 * 2**20, transcendentals=0),
        name="attend_back",
    )(qbits, kbits, q, *k, *v, g, o, ext, ktag, *inputs, *kept, *after)


def project_kernel(x, w_key, w_value, b_value, *refs):
    k_ref, v_ref = refs[-2:]
    k_ref[...] = mm(x[...], w_key[...], NN).astype(BF16)
    v_ref[...] = (mm(x[...], w_value[...], NN) + b_value[...].reshape(1, -1)).astype(BF16)
    if len(refs) > 2:
        w_query, b_query, q_ref = refs[:3]
        q_ref[...] = (mm(x[...], w_query[...], NN) + b_query[...].reshape(1, -1)).astype(BF16)


def project(x, w_key, w_value, b_value, *query):
    rows, d = x.shape
    tr = rows // 2
    tile = pl.BlockSpec((tr, d), lambda i: (i, 0))
    whole = pl.BlockSpec((d, d), lambda i: (0, 0), pipeline_mode=pl.Buffered(1))
    flat = pl.BlockSpec((d,), lambda i: (0,))
    outs = 3 if query else 2
    return pl.pallas_call(
        project_kernel,
        grid=(rows // tr,),
        in_specs=[tile, whole, whole, flat] + [whole, flat] * (outs - 2),
        out_specs=[tile] * outs,
        out_shape=[jax.ShapeDtypeStruct((rows, d), BF16)] * outs,
        compiler_params=pltpu.CompilerParams(vmem_limit_bytes=VMEM),
        cost_estimate=pl.CostEstimate(flops=6 * rows * d * d, bytes_accessed=10 * rows * d, transcendentals=0),
        name="project",
    )(x, w_key, w_value, b_value, *query)


def row_norm(values):
    centred = values - jnp.mean(values, axis=-1, keepdims=True)
    rstd = lax.rsqrt(jnp.mean(centred * centred, axis=-1, keepdims=True) + 1e-12)
    return centred * rstd, rstd


def norm_back(cot, gain, normed, rstd):
    e = cot * gain
    return rstd * (e - jnp.mean(e, axis=-1, keepdims=True) - normed * jnp.mean(e * normed, axis=-1, keepdims=True))


def dense_kernel(tf, hidden, mixed, out_grad, mask, w_out, w_up, w_down, b_out, gain_one, shift_one, b_up, b_down,
                 gain_two, shift_two, result, low_t, mixed_t, d_branch_t, active, d_upper, d_one, d_att, d_mixed, sums, slope,
                 sum_up):
    ff = w_up.shape[1]

    @pl.when(pl.program_id(0) == 0)
    def _():
        sums[...] = jnp.zeros_like(sums)
        sum_up[...] = jnp.zeros_like(sum_up)

    vec = lambda ref: ref[...].reshape(1, -1)
    r1 = hidden[...].astype(F32) + (mm(mixed[...], w_out[...], NN) + vec(b_out))
    n1, s1 = row_norm(r1)
    normed_one = n1 * vec(gain_one) + vec(shift_one)
    low = normed_one.astype(BF16)
    low_t[...] = low.T
    mixed_t[...] = mixed[...].T
    branch = jnp.zeros_like(r1)
    bias = vec(b_up)
    for t in range(0, ff, tf):
        c = pl.ds(t, tf)
        u = mm(low, w_up[:, c], NN) + bias[:, t:t + tf]
        phi = 0.5 + 0.5 * lax.erf(u * (0.5**0.5))
        a = (u * phi).astype(BF16)
        active[:, c] = a
        slope[:, c] = phi + u * (jnp.exp(u * u * -0.5) * 0.3989422804014327)
        branch = branch + mm(a, w_down[c, :], NN)
    n2, s2 = row_norm(normed_one + (branch + vec(b_down)))
    result[...] = (n2 * vec(gain_two) + vec(shift_two)).astype(BF16)
    cot = out_grad[...].astype(F32) * mask[...]
    d_two = norm_back(cot, vec(gain_two), n2, s2)
    db = d_two.astype(BF16)
    d_branch_t[...] = db.T
    sums[0:1, :] += col_sum(cot * n2)
    sums[1:2, :] += col_sum(cot)
    sums[2:3, :] += col_sum(db.astype(F32))
    d_normed = d_two
    for t in range(0, ff, tf):
        c = pl.ds(t, tf)
        du = (mm(db, w_down[c, :], NT) * slope[:, c]).astype(BF16)
        d_upper[:, c] = du
        sum_up[:, c] += col_sum(du.astype(F32))
        d_normed = d_normed + mm(du, w_up[:, c], NT)
    sums[3:4, :] += col_sum(d_normed * n1)
    sums[4:5, :] += col_sum(d_normed)
    d1 = norm_back(d_normed, vec(gain_one), n1, s1)
    d_one[...] = d1
    da = d1.astype(BF16)
    d_att[...] = da
    sums[5:6, :] += col_sum(da.astype(F32))
    d_mixed[...] = mm(da, w_out[...], NT).astype(BF16)

    @pl.when(pl.program_id(0) == pl.num_programs(0) - 1)
    def _():
        d = hidden.shape[1]
        for i in range(ff // d):
            sums[8 + i:9 + i, :] = sum_up[:, i * d:(i + 1) * d]


def dense(hidden, mixed, out_grad, mask, w_out, w_up, w_down, b_out, gain_one, shift_one, b_up, b_down, gain_two,
          shift_two, tr=256, tf=768):
    rows, d = hidden.shape
    ff = w_up.shape[1]
    row = lambda n: pl.BlockSpec((tr, n), lambda i: (i, 0))
    whole = lambda a, b: pl.BlockSpec((a, b), lambda i: (0, 0), pipeline_mode=pl.Buffered(1))
    flat = lambda n: pl.BlockSpec((n,), lambda i: (0,))
    shape = jax.ShapeDtypeStruct
    low = shape((rows, d), BF16)
    return pl.pallas_call(
        functools.partial(dense_kernel, tf),
        grid=(rows // tr,),
        in_specs=[row(d), row(d), row(d), row(1), whole(d, d), whole(d, ff), whole(ff, d), flat(d), flat(d), flat(d),
                  flat(ff), flat(d), flat(d), flat(d)],
        out_specs=[row(d)] + [pl.BlockSpec((d, tr), lambda i: (0, i))] * 3 + [row(ff), row(ff), row(d), row(d), row(d),
                   pl.BlockSpec((16, d), lambda i: (0, 0))],
        out_shape=[low] + [shape((d, rows), BF16)] * 3 + [shape((rows, ff), BF16)] * 2 + [shape((rows, d), F32), low, low,
                   shape((16, d), F32)],
        scratch_shapes=[pltpu.VMEM((tr, ff), F32), pltpu.VMEM((1, ff), F32)],
        compiler_params=pltpu.CompilerParams(vmem_limit_bytes=VMEM),
        cost_estimate=pl.CostEstimate(flops=40 * 10**9, bytes_accessed=40 * 2**20, transcendentals=0),
        name="dense",
    )(hidden, mixed, out_grad, mask.astype(F32).reshape(-1, 1), w_out, w_up, w_down, b_out, gain_one, shift_one, b_up,
      b_down, gain_two, shift_two)


def back_kernel(dk, dv, w_key, w_value, *refs):
    total = mm(dk[...], w_key[...], NT) + mm(dv[...], w_value[...], NT)
    if len(refs) > 1:
        dq, w_query, d_one, mate_part, far_part = refs[:5]
        total = total + mm(dq[...], w_query[...], NT) + d_one[...]
        total = total + mate_part[...].astype(F32) + far_part[...].astype(F32)
    refs[-1][...] = total.astype(BF16)


def back_product(band, dk, dv, w_key, w_value, own=()):
    d = w_key.shape[0]
    rows = dk.shape[0] // 3
    tr = rows // 2
    at = lambda i: (band * (rows // tr) + i, 0)
    row = lambda place: pl.BlockSpec((tr, d), place)
    whole = pl.BlockSpec((d, d), lambda i: (0, 0), pipeline_mode=pl.Buffered(1))
    first = lambda i: (i, 0)
    return pl.pallas_call(
        back_kernel,
        grid=(rows // tr,),
        in_specs=[row(at), row(at), whole, whole] + ([row(first), whole] + [row(first)] * 3 if own else []),
        out_specs=row(first),
        out_shape=jax.ShapeDtypeStruct((rows, d), BF16),
        compiler_params=pltpu.CompilerParams(vmem_limit_bytes=VMEM),
        cost_estimate=pl.CostEstimate(flops=(6 if own else 4) * rows * d * d, bytes_accessed=10 * rows * d, transcendentals=0),
        name="back_product",
    )(dk, dv, w_key, w_value, *own)


ALL = ("page", "band")


def everyone():
    return lax.axis_size("page") * lax.axis_size("band")


def swapped(block, mask):
    return lax.ppermute(block, ALL, [(i, i ^ mask) for i in range(everyone())])


def side(bit):
    return lax.rem(lax.div(lax.axis_index(ALL), bit), 2)


def masks_of(bits):
    masks = [0]
    for bit in reversed(bits):
        masks = masks + [mask | bit for mask in masks]
    return masks


def place_of(bits):
    at = 0
    for bit in bits:
        at = 2 * at + side(bit)
    return at


def dealt(block, bits, axis):
    masks = masks_of(bits)
    size = block.shape[axis] // len(masks)
    place = place_of(bits)
    return [lax.dynamic_slice_in_dim(block, jnp.bitwise_xor(place, i) * size, size, axis) for i in range(len(masks))]


def sent(parts, bits):
    return [swapped(part, mask) for part, mask in zip(parts, masks_of(bits)[1:])]


def summed(parts):
    parts = [part.astype(F32) for part in parts]
    while len(parts) > 1:
        parts = [parts[i] + parts[i + 1] for i in range(0, len(parts), 2)]
    return parts[0].astype(BF16)


class Summing:
    def __init__(self, parts, stages):
        self.stages, self.at = stages, 0
        self.parts = parts

    def advance(self, held=None):
        if self.at < len(self.stages):
            theirs = sent(self.parts[1:], self.stages[self.at])
            if held is not None:
                theirs, held = lax.optimization_barrier((theirs, held))
            block = summed([self.parts[0]] + theirs)
            self.at += 1
            self.parts = dealt(block, self.stages[self.at], 0) if self.at < len(self.stages) else [block]
        return held


def in_order(parts, bits):
    for i, bit in enumerate(bits):
        far = 1 << (len(bits) - 1 - i)
        flip = side(bit) == 1
        parts = [jnp.where(flip, parts[j ^ far], parts[j]) for j in range(len(parts))]
    return jnp.concatenate(parts)


def products_kernel(low, mixed, d_branch, d_upper, d_att, active, made):
    step = pl.program_id(0)
    count = (pl.num_programs(0) - 1) // 2
    middle = (step >= count) & (step < 2 * count)
    for here, left, right in ((step < count, d_branch, active), (middle, low, d_upper), (step == 2 * count, mixed, d_att)):
        @pl.when(here)
        def _():
            made[...] = mm(left[...], right[...], NN).astype(BF16)


def feed_forward_products(low, mixed, d_branch, d_upper, d_att, active):
    d, rows = low.shape
    count = active.shape[1] // d
    once = lambda n, m: pl.BlockSpec((n, m), lambda j: (0, 0), pipeline_mode=pl.Buffered(1))
    along = lambda first: pl.BlockSpec((rows, d), lambda j: (0, jnp.clip(j - first, 0, count - 1)))
    return pl.pallas_call(
        products_kernel,
        grid=(2 * count + 1,),
        in_specs=[once(d, rows)] * 3 + [along(count), once(rows, d), along(0)],
        out_specs=pl.BlockSpec((d, d), lambda j: (0, j)),
        out_shape=jax.ShapeDtypeStruct((d, (2 * count + 1) * d), BF16),
        compiler_params=pltpu.CompilerParams(vmem_limit_bytes=VMEM),
        cost_estimate=pl.CostEstimate(flops=2 * rows * d * d * (2 * count + 1), bytes_accessed=20 * d * d * count,
                                      transcendentals=0),
        name="products",
    )(low, mixed, d_branch, d_upper, d_att, active)


def place_kernel(from_down, from_up, from_out, down, up, out):
    down[...] = from_down[...].T.astype(F32)
    up[...] = from_up[...].astype(F32)
    out[...] = from_out[...].astype(F32)


def feed_forward_whole(got):
    d = got.shape[0]
    ff = (got.shape[1] - d) // 2
    steps = d // PAIR
    row = lambda n: pl.BlockSpec((PAIR, n), lambda j: (j, 0))
    return pl.pallas_call(
        place_kernel,
        grid=(steps,),
        in_specs=[pl.BlockSpec((d, ff // steps), lambda j: (0, j)), pl.BlockSpec((PAIR, ff), lambda j: (j, 1)),
                  pl.BlockSpec((PAIR, d), lambda j: (j, 2 * ff // d))],
        out_specs=[pl.BlockSpec((ff // steps, d), lambda j: (j, 0)), row(ff), row(d)],
        out_shape=[jax.ShapeDtypeStruct(shape, F32) for shape in ((ff, d), (d, ff), (d, d))],
        compiler_params=pltpu.CompilerParams(vmem_limit_bytes=VMEM),
        cost_estimate=pl.CostEstimate(flops=0, bytes_accessed=12 * ff * d, transcendentals=0),
        name="place",
    )(got, got, got)


def split_kernel(x, q, k, v):
    for i, out in enumerate((q, k, v)):
        for p in range(q.shape[1] // PAIR):
            at = (3 * p + i) * PAIR
            out[:, p * PAIR:(p + 1) * PAIR] = x[:, at:at + PAIR].astype(F32)


def split_projections(x):
    d = x.shape[0]
    tr = d // 3
    row = lambda n: pl.BlockSpec((tr, n), lambda i: (i, 0))
    return pl.pallas_call(
        split_kernel,
        grid=(3,),
        in_specs=[row(3 * d)],
        out_specs=[row(d)] * 3,
        out_shape=[jax.ShapeDtypeStruct((d, d), F32)] * 3,
        compiler_params=pltpu.CompilerParams(vmem_limit_bytes=32 * 2**20),
        cost_estimate=pl.CostEstimate(flops=0, bytes_accessed=18 * d * d, transcendentals=0),
        name="split",
    )(x)


def tag_columns(page_ids, near_tags):
    place = jnp.arange(PAIR)[None, :] % HEAD
    qtag = jnp.where(jnp.arange(PAIR)[None, :] == page_ids[:, None], 1.0, 0.0).astype(BF16)
    ktag = jnp.where((place < 2) & (near_tags[:, None] != place + 1), BLOCKED, 0.0)
    return qtag, jnp.where((place >= 2) & (place < 5), -1.0, ktag).astype(BF16)


def tokens_of(near_tags, rows):
    have = jnp.sum((near_tags.reshape(-1, rows) > 0).astype(jnp.int32), axis=1)
    return (have + (TILE - 1)) // TILE


def tile_bits(tags, tile):
    tags = tags.reshape(-1, tile)
    return sum(jnp.max(jnp.where(tags == d + 1, 1 << d, 0), axis=1) for d in range(2)).astype(jnp.int32)


def body(hidden, page_ids, key_mask, out_grad, w_query, b_query, w_key, w_value, b_value, w_out, b_out, gain_one,
         shift_one, w_up, b_up, w_down, b_down, gain_two, shift_two):
    rows, d = hidden.shape
    bands = lax.axis_size("band")
    mates = [(i, i ^ 1) for i in range(bands)]
    across = [(i, i + 1) for i in range(1, bands - 1, 2)] + [(i + 1, i) for i in range(1, bands - 1, 2)]
    to_mate = lambda x: lax.ppermute(x, "band", mates)
    to_across = lambda x: lax.ppermute(x, "band", across)

    key_tags = jnp.where(key_mask == 1, page_ids + 1, 0)
    far, mate = to_across(hidden), to_mate(hidden)
    near_tags = jnp.concatenate([key_tags, to_mate(key_tags), to_across(key_tags)])
    queries, *own_pair = project(hidden, w_key, w_value, b_value, w_query, b_query)
    mate_pair, far_pair = project(mate, w_key, w_value, b_value), project(far, w_key, w_value, b_value)
    keys, values = zip(own_pair, mate_pair, far_pair)
    qtag, ktag = tag_columns(page_ids, near_tags)
    tk = 512
    tokens, qbits, kbits = tokens_of(near_tags, rows), tile_bits(key_tags, TILE), tile_bits(near_tags, tk)
    tokens, qbits, kbits, queries = lax.optimization_barrier((tokens, qbits, kbits, queries))

    mixed, ext = attend(queries, keys, values, qtag, ktag, tokens)
    (result, low_t, mixed_t, d_branch_t, active, d_upper, d_one, d_att, d_mixed, sums) = dense(
        hidden, mixed, out_grad, key_mask, w_out, w_up, w_down, b_out, gain_one, shift_one, b_up, b_down, gain_two,
        shift_two)

    count = everyone().bit_length() - 1
    core, y, x, z = 1, 2, bands, 2 * bands
    rest = [1 << i for i in range(count) if 1 << i not in (core, y, x, z)]
    direct = [[core], [x, y]] + [([z] + rest)[i:i + 2] for i in range(0, 1 + len(rest), 2)]

    products = feed_forward_products(low_t, mixed_t, d_branch_t, d_upper, d_att, active)
    products, d_mixed = lax.optimization_barrier((products, d_mixed))
    shares = lax.psum_scatter(products, ALL, scatter_dimension=0, tiled=True)

    pairs = d // PAIR
    kept, made, at, after = (sums,), [], 0, []
    for size in (2, 2, pairs - 4):
        *kept, made_now = attend_back(at, size, kept, after, queries, keys, values, d_mixed, mixed, ext, ktag,
                                      (hidden, mate, far), qbits, kbits, tk)
        at += size
        made.append(made_now)
        if at == 2:
            early = Summing(dealt(made[0], [core], 0), direct[:2])
            after = early.parts
        elif at == 4:
            kept[1] = early.advance(kept[1])
            late = Summing(dealt(made[1], [core], 0), direct[:1])
            after = early.parts + late.parts
    for stream in (early, late):
        kept[1] = stream.advance(kept[1])
    vectors, dq, dk, dv = kept

    keep, send = dealt(made[-1], [core], 0)
    vectors = vectors.astype(BF16)
    dk, send = lax.optimization_barrier((dk, send))
    theirs = [swapped(send, core), swapped(vectors, core)]
    far_part = back_product(2, dk, dv, w_key, w_value)
    theirs, far_part = lax.optimization_barrier((theirs, far_part))
    far_part = to_across(far_part)
    block = jnp.concatenate([late.parts[0], summed([keep, theirs[0]])], axis=1)
    vectors = summed([vectors, theirs[1]])
    vectors = jnp.concatenate([vectors[:8], vectors[8:]], axis=1)
    for i, bits in enumerate(direct[1:]):
        parts = dealt(block, bits, 0)
        send = [jnp.concatenate([part, vectors]) for part in parts[1:]]
        if i == 0:
            send, dk = lax.optimization_barrier((send, dk))
        theirs = sent(send, bits)
        if i == 0:
            shares, dk = lax.optimization_barrier((shares, dk))
            got = lax.all_gather(shares, ALL, axis=0, tiled=True)
            mate_part = back_product(1, dk, dv, w_key, w_value)
            theirs, mate_part = lax.optimization_barrier((theirs, mate_part))
            mate_part = to_mate(mate_part)
        elif i == 1:
            input_grad = back_product(0, dk, dv, w_key, w_value, (dq, w_query, d_one, mate_part, far_part))
            theirs, input_grad = lax.optimization_barrier((theirs, input_grad))
        size = parts[0].shape[0]
        block = summed([parts[0]] + [other[:size] for other in theirs])
        vectors = summed([vectors] + [other[size:] for other in theirs])
        if i == 0:
            block = jnp.concatenate([early.parts[0], block], axis=1)
            vectors = jnp.pad(vectors, ((0, 0), (0, block.shape[1] - vectors.shape[1])))
    vectors = jnp.concatenate([vectors[:, :d], vectors[:, d:2 * d]]).astype(F32)

    for bits in reversed(direct):
        theirs = sent([block] * (len(masks_of(bits)) - 1), bits)
        block = in_order([block] + theirs, bits)
    grad_query, grad_key, grad_value = split_projections(block)
    got, grad_query = lax.optimization_barrier((got, grad_query))
    grad_down, grad_up, grad_out = feed_forward_whole(got)
    return (
        result,
        input_grad,
        grad_query,
        vectors[12],
        grad_key,
        grad_value,
        vectors[13],
        grad_out,
        vectors[5],
        vectors[3],
        vectors[4],
        grad_up,
        vectors[8:12].reshape(-1),
        grad_down,
        vectors[2],
        vectors[0],
        vectors[1],
    )


def solution(mesh):
    split = P(("page", "band"), None)
    line = P(("page", "band"))
    return jax.shard_map(
        body,
        mesh=mesh,
        in_specs=(split, line, line, split) + (P(),) * 15,
        out_specs=(split, split) + (P(),) * 15,
        check_vma=False,
    )
```

```python
import functools

import jax
import jax.numpy as jnp
from jax import lax
from jax.experimental import pallas as pl
from jax.experimental.pallas import tpu as pltpu
from jax.sharding import PartitionSpec as P


HEAD = 64
PAIR = 128
BLOCKED = -1e30
SAFE = 60.0
SOME_VMEM = 48 * 2**20
VMEM = 60 * 2**20
NT = (((1,), (1,)), ((), ()))
NN = (((1,), (0,)), ((), ()))
TN = (((0,), (0,)), ((), ()))
F32 = jnp.float32
BF16 = jnp.bfloat16
SCALE = HEAD**-0.5
TILE = 256


def mm(a, b, dims):
    return lax.dot_general(a, b, dims, preferred_element_type=F32)


def col_sum(x):
    return jnp.sum(x, axis=0, keepdims=True)


def tile_at(i, tile=TILE):
    return pl.ds(pl.multiple_of(i * tile, tile), tile)


def parts(x):
    hi = x.astype(BF16)
    rest = x - hi.astype(F32)
    mid = rest.astype(BF16)
    return hi, mid, (rest - mid.astype(F32)).astype(BF16)


def same_half():
    a, b = (lax.broadcasted_iota(jnp.int32, (PAIR, PAIR), i) < HEAD for i in (0, 1))
    return jnp.where(a == b, 1.0, 0.0).astype(BF16)


def left_lanes():
    return lax.broadcasted_iota(jnp.int32, (1, PAIR), 1) < HEAD


def together(bands, whole):
    rows = bands[0].shape[0]
    for i, band in enumerate(bands):
        whole[i * rows:(i + 1) * rows, :] = band[...]


def attend_kernel(tiles, q_ref, k_own, k_mate, k_far, v_own, v_mate, v_far, qtag_ref, ktag_ref, o_ref, ext_ref,
                  kx, qx0, qx1, vt, acc0, acc1, top0, top1):
    rows, near = q_ref.shape[0], ktag_ref.shape[0]
    left = left_lanes()
    q_pair = q_ref[...] * jnp.asarray(SCALE, BF16)
    zero = jnp.zeros_like(q_pair)
    qx0[:, :PAIR] = jnp.where(left, q_pair, zero)
    qx1[:, :PAIR] = jnp.where(left, zero, q_pair)
    qx0[:, PAIR:] = qtag_ref[...]
    qx1[:, PAIR:] = qtag_ref[...]
    kx[:, PAIR:] = ktag_ref[...]
    vt[HEAD:PAIR, :] = jnp.ones((HEAD, near), BF16)
    halves = same_half()

    def longest(x):
        x = x.astype(F32)
        return jnp.max(mm((x * x).astype(BF16), halves, NN), axis=0, keepdims=True)

    reach = 0.0
    for i, (k_band, v_band) in enumerate(((k_own, v_own), (k_mate, v_mate), (k_far, v_far))):
        span = slice(i * rows, (i + 1) * rows)
        kx[span, :PAIR] = k_band[...]
        turned = v_band[...].T
        vt[:HEAD, span] = turned[:HEAD]
        vt[PAIR:, span] = turned[HEAD:]
        reach = jnp.maximum(reach, longest(k_band[...]))
    plain = jnp.max(reach * longest(q_pair)) < (SAFE * 0.98) ** 2
    heads = ((acc0, top0, qx0, slice(0, PAIR)), (acc1, top1, qx1, slice(HEAD, HEAD + PAIR)))
    for acc, *_ in heads:
        acc[...] = jnp.zeros_like(acc)

    @pl.when(plain)
    def _():
        for _, top, *_ in heads:
            top[...] = jnp.zeros_like(top)

        def per_band(band, _):
            for n in range(1, rows // TILE + 1):
                @pl.when(tiles[band] == n)
                def _():
                    ks = pl.ds(pl.multiple_of(band * rows, rows), n * TILE)
                    scores = [mm(kx[ks, :], qx[...], NT) for _, _, qx, _ in heads]
                    probs = [jnp.exp(s).astype(BF16) for s in scores]
                    for (acc, _, _, at), p in zip(heads, probs):
                        acc[...] += mm(vt[at, ks], p, NN)
            return 0

        lax.fori_loop(0, near // rows, per_band, 0)

    @pl.when(jnp.logical_not(plain))
    def _():
        for _, top, *_ in heads:
            top[...] = jnp.full_like(top, -3e38)

        def per_k(ki, _):
            @pl.when(lax.rem(ki, rows // TILE) < tiles[lax.div(ki, rows // TILE)])
            def _():
                ks = tile_at(ki)
                for acc, top, qx, at in heads:
                    s = mm(kx[ks, :], qx[...], NT)
                    old = top[...]
                    new = jnp.maximum(old, jnp.max(s, axis=0, keepdims=True))
                    p = jnp.exp(s - new[:1, :]).astype(BF16)
                    acc[...] = acc[...] * jnp.exp(old - new)[:1, :] + mm(vt[at, ks], p, NN)
                    top[...] = new
            return 0

        lax.fori_loop(0, near // TILE, per_k, 0)

    def finish(qi, _):
        qs = tile_at(qi)
        tags = qtag_ref[qs, :].astype(F32).T[:8]
        place = lax.broadcasted_iota(jnp.int32, (8, TILE), 0)
        out, ext = [], []
        for acc, top, _, at in heads:
            total, plain_out = (acc[HEAD:, qs], acc[:HEAD, qs]) if at.start == 0 else (acc[:HEAD, qs], acc[HEAD:, qs])
            out.append(plain_out / total)
            hi, mid, lo = (x.astype(F32) for x in parts(jnp.log(total[:8]) + top[:, qs]))
            head = jnp.where(place == 2, hi, jnp.where(place == 3, mid, jnp.where(place == 4, lo, tags)))
            ext += [head, jnp.zeros((HEAD - 8, TILE), F32)]
        o_ref[qs, :] = jnp.concatenate(out, axis=0).T.astype(BF16)
        ext_ref[qs, :] = jnp.concatenate(ext, axis=0).T.astype(BF16)
        return 0

    lax.fori_loop(0, rows // TILE, finish, 0)


def attend(q, k, v, qtag, ktag, tiles):
    rows, d = q.shape
    near = len(k) * rows
    part = lambda n: pl.BlockSpec((n, PAIR), lambda p, *_: (0, p))
    fixed = lambda n: pl.BlockSpec((n, PAIR), lambda p, *_: (0, 0))
    return pl.pallas_call(
        attend_kernel,
        grid_spec=pltpu.PrefetchScalarGridSpec(
            num_scalar_prefetch=1,
            grid=(d // PAIR,),
            in_specs=[part(rows)] + [part(rows)] * 6 + [fixed(rows), fixed(near)],
            out_specs=[part(rows)] * 2,
            scratch_shapes=[pltpu.VMEM((n, 2 * PAIR), BF16) for n in (near, rows, rows)] + [pltpu.VMEM((PAIR + HEAD, near), BF16)]
            + [pltpu.VMEM((PAIR, rows), F32)] * 2 + [pltpu.VMEM((8, rows), F32)] * 2,
        ),
        out_shape=[jax.ShapeDtypeStruct((rows, d), BF16)] * 2,
        compiler_params=pltpu.CompilerParams(vmem_limit_bytes=VMEM),
        cost_estimate=pl.CostEstimate(flops=40 * 10**9, bytes_accessed=16 * 2**20, transcendentals=0),
        name="attend",
    )(tiles, q, *k, *v, qtag, ktag)


def hull(qbits, want, nq):
    first, last = jnp.int32(nq), jnp.int32(0)
    for qi in reversed(range(nq)):
        hit = (qbits[qi] & want) != 0
        last = jnp.where(hit & (last == 0), qi + 1, last)
        first = jnp.where(hit, qi, first)
    return first, jnp.maximum(last - first, 0)


def attend_back_kernel(tk, qbits, kbits, q_ref, k_own, k_mate, k_far, v_own, v_mate, v_far, g_ref, o_ref, ext_ref, ktag_ref,
                       own_in, mate_in, far_in, sums_in, *refs):
    (sums, dq_ref, dk_ref, dv_ref, w_ref, k_ref, v_ref, qx0, qx1, gx0, gx1, qt, gt, dq_acc, dk_acc, dv_acc, own_ref, mate_ref,
     far_ref, arrived) = refs[-20:]
    rows, near = q_ref.shape[0], k_ref.shape[0]
    first = pl.program_id(0) == 0
    copies = [pltpu.make_async_copy(a, b, arrived.at[i])
              for i, (a, b) in enumerate(((own_in, own_ref), (mate_in, mate_ref), (far_in, far_ref)))]

    @pl.when(first)
    def _():
        for copy in copies:
            copy.start()

    together((k_own, k_mate, k_far), k_ref)
    together((v_own, v_mate, v_far), v_ref)
    nq = rows // TILE
    left = left_lanes()
    place = lax.broadcasted_iota(jnp.int32, (1, PAIR), 1) % HEAD
    halves = same_half()

    def per_q(qi, _):
        qs = tile_at(qi)
        q_pair, g_pair, ext = q_ref[qs, :], g_ref[qs, :], ext_ref[qs, :]
        qt[:, qs] = q_pair.T
        gt[:, qs] = g_pair.T
        zero = jnp.zeros_like(q_pair)
        hi, mid, _ = parts(g_pair.astype(F32) * o_ref[qs, :].astype(F32))
        hi, mid, _ = parts(mm(hi, halves, NN) + mm(mid, halves, NN))
        inner = jnp.where(place == 2, hi, jnp.where(place == 3, mid, zero))
        scaled = q_pair * jnp.asarray(SCALE, BF16)
        for x0, x1, base, more in ((qx0, qx1, scaled, ext), (gx0, gx1, g_pair, inner)):
            x0[qs, :PAIR] = jnp.where(left, base, zero)
            x1[qs, :PAIR] = jnp.where(left, zero, base)
            x0[qs, PAIR:] = jnp.where(left, more, zero)
            x1[qs, PAIR:] = jnp.where(left, zero, more)
        return 0

    lax.fori_loop(0, nq, per_q, 0)
    dq_acc[...] = jnp.zeros_like(dq_acc)

    def per_k(ki, _):
        first, count = hull(qbits, kbits[ki], nq)
        ks = tile_at(ki, tk)

        @pl.when(count == 0)
        def _():
            dk_acc[:, ks] = jnp.zeros((PAIR, tk), F32)
            dv_acc[:, ks] = jnp.zeros((PAIR, tk), F32)

        for n in range(1, nq + 1):
            @pl.when(count == n)
            def _():
                qs = pl.ds(pl.multiple_of(first * TILE, TILE), n * TILE)
                k_pair, tags = k_ref[ks, :], ktag_ref[ks, :]
                zero = jnp.zeros_like(k_pair)
                kx = jnp.concatenate([k_pair, tags], axis=1)
                vx = jnp.concatenate([v_ref[ks, :], tags], axis=1)
                s0 = mm(qx0[qs, :], kx, NT)
                d0 = mm(gx0[qs, :], vx, NT)
                p0 = jnp.exp(s0)
                s1 = mm(qx1[qs, :], kx, NT)
                ds0 = (p0 * d0).astype(BF16)
                p0 = p0.astype(BF16)
                d1 = mm(gx1[qs, :], vx, NT)
                p1 = jnp.exp(s1)
                dv_acc[:HEAD, ks] = mm(gt[:HEAD, qs], p0, NN)
                dk_acc[:HEAD, ks] = mm(qt[:HEAD, qs], ds0, NN)
                ds1 = (p1 * d1).astype(BF16)
                p1 = p1.astype(BF16)
                dq = mm(ds0, jnp.where(left, k_pair, zero), NN)
                dv_acc[HEAD:, ks] = mm(gt[HEAD:, qs], p1, NN)
                dk_acc[HEAD:, ks] = mm(qt[HEAD:, qs], ds1, NN)
                dq = dq + mm(ds1, jnp.where(left, zero, k_pair), NN)
                dq_acc[qs, :] += dq
        return 0

    lax.fori_loop(0, near // tk, per_k, 0)
    dq = (dq_acc[...] * SCALE).astype(BF16)
    dk = (dk_acc[...] * SCALE).astype(BF16)
    dv = dv_acc[...].astype(BF16)
    dq_ref[...] = dq
    dk_ref[...] = dk.T
    dv_ref[...] = dv.T

    @pl.when(first)
    def _():
        for copy in copies:
            copy.wait()

    w_ref[:, :PAIR] = mm(dq, own_ref[...], TN).T.astype(BF16)
    for i, x in ((1, dk), (2, dv)):
        total = mm(x[:, :rows], own_ref[...], NN)
        total = total + mm(x[:, rows:2 * rows], mate_ref[...], NN)
        total = total + mm(x[:, 2 * rows:], far_ref[...], NN)
        w_ref[:, i * PAIR:(i + 1) * PAIR] = total.T.astype(BF16)
    row = lax.broadcasted_iota(jnp.int32, (8, PAIR), 0)
    by_column = lambda ref: mm(jnp.ones((8, ref.shape[0]), BF16), ref[...], NN)
    sums[...] = jnp.where(row == 4, by_column(dq_ref), jnp.where(row == 5, by_column(dv_ref), sums_in[...]))


def attend_back(pair, pairs, kept, after, q, k, v, g, o, ext, ktag, inputs, qbits, kbits, tk):
    rows, d = q.shape
    near = len(k) * rows
    part = lambda n: pl.BlockSpec((n, PAIR), lambda p, *_: (0, pair + p))
    once = lambda n, m: pl.BlockSpec((n, m), lambda p, *_: (0, 0), pipeline_mode=pl.Buffered(1))
    sums = pl.BlockSpec((8, PAIR), lambda p, *_: (1, pair + p))
    hold = pl.BlockSpec(memory_space=pl.ANY)
    return pl.pallas_call(
        functools.partial(attend_back_kernel, tk),
        grid_spec=pltpu.PrefetchScalarGridSpec(
            num_scalar_prefetch=2,
            grid=(pairs,),
            in_specs=[part(rows)] * 10 + [once(near, PAIR)] + [hold] * 3 + [sums]
            + [hold] * (len(kept) - 1 + len(after)),
            out_specs=[sums, part(rows), part(near), part(near), pl.BlockSpec((d, 3 * PAIR), lambda p, *_: (0, p))],
            scratch_shapes=[pltpu.VMEM((near, PAIR), BF16)] * 2 + [pltpu.VMEM((rows, 2 * PAIR), BF16)] * 4
            + [pltpu.VMEM((PAIR, rows), BF16)] * 2 + [pltpu.VMEM((rows, PAIR), F32)] + [pltpu.VMEM((PAIR, near), F32)] * 2
            + [pltpu.VMEM((rows, d), BF16)] * 3 + [pltpu.SemaphoreType.DMA((3,))],
        ),
        out_shape=[jax.ShapeDtypeStruct((16, d), F32)] + [jax.ShapeDtypeStruct((n, d), BF16) for n in (rows, near, near)]
        + [jax.ShapeDtypeStruct((d, pairs * 3 * PAIR), BF16)],
        input_output_aliases={16 + i: i for i in range(len(kept))},
        compiler_params=pltpu.CompilerParams(vmem_limit_bytes=SOME_VMEM),
        cost_estimate=pl.CostEstimate(flops=18 * pairs * 10**9, bytes_accessed=8 * 2**20, transcendentals=0),
        name="attend_back",
    )(qbits, kbits, q, *k, *v, g, o, ext, ktag, *inputs, *kept, *after)


def project_kernel(x, w_key, w_value, b_value, *refs):
    k_ref, v_ref = refs[-2:]
    k_ref[...] = mm(x[...], w_key[...], NN).astype(BF16)
    v_ref[...] = (mm(x[...], w_value[...], NN) + b_value[...].reshape(1, -1)).astype(BF16)
    if len(refs) > 2:
        w_query, b_query, q_ref = refs[:3]
        q_ref[...] = (mm(x[...], w_query[...], NN) + b_query[...].reshape(1, -1)).astype(BF16)


def project(x, w_key, w_value, b_value, *query):
    rows, d = x.shape
    tr = rows // 2
    tile = pl.BlockSpec((tr, d), lambda i: (i, 0))
    whole = pl.BlockSpec((d, d), lambda i: (0, 0), pipeline_mode=pl.Buffered(1))
    flat = pl.BlockSpec((d,), lambda i: (0,))
    outs = 3 if query else 2
    return pl.pallas_call(
        project_kernel,
        grid=(rows // tr,),
        in_specs=[tile, whole, whole, flat] + [whole, flat] * (outs - 2),
        out_specs=[tile] * outs,
        out_shape=[jax.ShapeDtypeStruct((rows, d), BF16)] * outs,
        compiler_params=pltpu.CompilerParams(vmem_limit_bytes=VMEM),
        cost_estimate=pl.CostEstimate(flops=6 * rows * d * d, bytes_accessed=10 * rows * d, transcendentals=0),
        name="project",
    )(x, w_key, w_value, b_value, *query)


def row_norm(values):
    centred = values - jnp.mean(values, axis=-1, keepdims=True)
    rstd = lax.rsqrt(jnp.mean(centred * centred, axis=-1, keepdims=True) + 1e-12)
    return centred * rstd, rstd


def norm_back(cot, gain, normed, rstd):
    e = cot * gain
    return rstd * (e - jnp.mean(e, axis=-1, keepdims=True) - normed * jnp.mean(e * normed, axis=-1, keepdims=True))


def dense_kernel(tf, hidden, mixed, out_grad, mask, w_out, w_up, w_down, b_out, gain_one, shift_one, b_up, b_down,
                 gain_two, shift_two, result, low_t, mixed_t, d_branch_t, active, d_upper, d_one, d_att, d_mixed, sums, slope,
                 sum_up):
    ff = w_up.shape[1]

    @pl.when(pl.program_id(0) == 0)
    def _():
        sums[...] = jnp.zeros_like(sums)
        sum_up[...] = jnp.zeros_like(sum_up)

    vec = lambda ref: ref[...].reshape(1, -1)
    r1 = hidden[...].astype(F32) + (mm(mixed[...], w_out[...], NN) + vec(b_out))
    n1, s1 = row_norm(r1)
    normed_one = n1 * vec(gain_one) + vec(shift_one)
    low = normed_one.astype(BF16)
    low_t[...] = low.T
    mixed_t[...] = mixed[...].T
    branch = jnp.zeros_like(r1)
    bias = vec(b_up)
    for t in range(0, ff, tf):
        c = pl.ds(t, tf)
        u = mm(low, w_up[:, c], NN) + bias[:, t:t + tf]
        phi = 0.5 + 0.5 * lax.erf(u * (0.5**0.5))
        a = (u * phi).astype(BF16)
        active[:, c] = a
        slope[:, c] = phi + u * (jnp.exp(u * u * -0.5) * 0.3989422804014327)
        branch = branch + mm(a, w_down[c, :], NN)
    n2, s2 = row_norm(normed_one + (branch + vec(b_down)))
    result[...] = (n2 * vec(gain_two) + vec(shift_two)).astype(BF16)
    cot = out_grad[...].astype(F32) * mask[...]
    d_two = norm_back(cot, vec(gain_two), n2, s2)
    db = d_two.astype(BF16)
    d_branch_t[...] = db.T
    sums[0:1, :] += col_sum(cot * n2)
    sums[1:2, :] += col_sum(cot)
    sums[2:3, :] += col_sum(db.astype(F32))
    d_normed = d_two
    for t in range(0, ff, tf):
        c = pl.ds(t, tf)
        du = (mm(db, w_down[c, :], NT) * slope[:, c]).astype(BF16)
        d_upper[:, c] = du
        sum_up[:, c] += col_sum(du.astype(F32))
        d_normed = d_normed + mm(du, w_up[:, c], NT)
    sums[3:4, :] += col_sum(d_normed * n1)
    sums[4:5, :] += col_sum(d_normed)
    d1 = norm_back(d_normed, vec(gain_one), n1, s1)
    d_one[...] = d1
    da = d1.astype(BF16)
    d_att[...] = da
    sums[5:6, :] += col_sum(da.astype(F32))
    d_mixed[...] = mm(da, w_out[...], NT).astype(BF16)

    @pl.when(pl.program_id(0) == pl.num_programs(0) - 1)
    def _():
        d = hidden.shape[1]
        for i in range(ff // d):
            sums[8 + i:9 + i, :] = sum_up[:, i * d:(i + 1) * d]


def dense(hidden, mixed, out_grad, mask, w_out, w_up, w_down, b_out, gain_one, shift_one, b_up, b_down, gain_two,
          shift_two, tr=256, tf=768):
    rows, d = hidden.shape
    ff = w_up.shape[1]
    row = lambda n: pl.BlockSpec((tr, n), lambda i: (i, 0))
    whole = lambda a, b: pl.BlockSpec((a, b), lambda i: (0, 0), pipeline_mode=pl.Buffered(1))
    flat = lambda n: pl.BlockSpec((n,), lambda i: (0,))
    shape = jax.ShapeDtypeStruct
    low = shape((rows, d), BF16)
    return pl.pallas_call(
        functools.partial(dense_kernel, tf),
        grid=(rows // tr,),
        in_specs=[row(d), row(d), row(d), row(1), whole(d, d), whole(d, ff), whole(ff, d), flat(d), flat(d), flat(d),
                  flat(ff), flat(d), flat(d), flat(d)],
        out_specs=[row(d)] + [pl.BlockSpec((d, tr), lambda i: (0, i))] * 3 + [row(ff), row(ff), row(d), row(d), row(d),
                   pl.BlockSpec((16, d), lambda i: (0, 0))],
        out_shape=[low] + [shape((d, rows), BF16)] * 3 + [shape((rows, ff), BF16)] * 2 + [shape((rows, d), F32), low, low,
                   shape((16, d), F32)],
        scratch_shapes=[pltpu.VMEM((tr, ff), F32), pltpu.VMEM((1, ff), F32)],
        compiler_params=pltpu.CompilerParams(vmem_limit_bytes=VMEM),
        cost_estimate=pl.CostEstimate(flops=40 * 10**9, bytes_accessed=40 * 2**20, transcendentals=0),
        name="dense",
    )(hidden, mixed, out_grad, mask.astype(F32).reshape(-1, 1), w_out, w_up, w_down, b_out, gain_one, shift_one, b_up,
      b_down, gain_two, shift_two)


def back_kernel(dk, dv, w_key, w_value, *refs):
    total = mm(dk[...], w_key[...], NT) + mm(dv[...], w_value[...], NT)
    if len(refs) > 1:
        dq, w_query, d_one, mate_part, far_part = refs[:5]
        total = total + mm(dq[...], w_query[...], NT) + d_one[...]
        total = total + mate_part[...].astype(F32) + far_part[...].astype(F32)
    refs[-1][...] = total.astype(BF16)


def back_product(band, dk, dv, w_key, w_value, own=()):
    d = w_key.shape[0]
    rows = dk.shape[0] // 3
    tr = rows // 2
    at = lambda i: (band * (rows // tr) + i, 0)
    row = lambda place: pl.BlockSpec((tr, d), place)
    whole = pl.BlockSpec((d, d), lambda i: (0, 0), pipeline_mode=pl.Buffered(1))
    first = lambda i: (i, 0)
    return pl.pallas_call(
        back_kernel,
        grid=(rows // tr,),
        in_specs=[row(at), row(at), whole, whole] + ([row(first), whole] + [row(first)] * 3 if own else []),
        out_specs=row(first),
        out_shape=jax.ShapeDtypeStruct((rows, d), BF16),
        compiler_params=pltpu.CompilerParams(vmem_limit_bytes=VMEM),
        cost_estimate=pl.CostEstimate(flops=(6 if own else 4) * rows * d * d, bytes_accessed=10 * rows * d, transcendentals=0),
        name="back_product",
    )(dk, dv, w_key, w_value, *own)


ALL = ("page", "band")


def everyone():
    return lax.axis_size("page") * lax.axis_size("band")


def swapped(block, mask):
    return lax.ppermute(block, ALL, [(i, i ^ mask) for i in range(everyone())])


def side(bit):
    return lax.rem(lax.div(lax.axis_index(ALL), bit), 2)


def masks_of(bits):
    masks = [0]
    for bit in reversed(bits):
        masks = masks + [mask | bit for mask in masks]
    return masks


def place_of(bits):
    at = 0
    for bit in bits:
        at = 2 * at + side(bit)
    return at


def dealt(block, bits, axis):
    masks = masks_of(bits)
    size = block.shape[axis] // len(masks)
    place = place_of(bits)
    return [lax.dynamic_slice_in_dim(block, jnp.bitwise_xor(place, i) * size, size, axis) for i in range(len(masks))]


def sent(parts, bits):
    return [swapped(part, mask) for part, mask in zip(parts, masks_of(bits)[1:])]


def summed(parts):
    parts = [part.astype(F32) for part in parts]
    while len(parts) > 1:
        parts = [parts[i] + parts[i + 1] for i in range(0, len(parts), 2)]
    return parts[0].astype(BF16)


class Summing:
    def __init__(self, parts, stages):
        self.stages, self.at = stages, 0
        self.parts = parts

    def advance(self, held=None):
        if self.at < len(self.stages):
            theirs = sent(self.parts[1:], self.stages[self.at])
            if held is not None:
                theirs, held = lax.optimization_barrier((theirs, held))
            block = summed([self.parts[0]] + theirs)
            self.at += 1
            self.parts = dealt(block, self.stages[self.at], 0) if self.at < len(self.stages) else [block]
        return held


def in_order(parts, bits):
    for i, bit in enumerate(bits):
        far = 1 << (len(bits) - 1 - i)
        flip = side(bit) == 1
        parts = [jnp.where(flip, parts[j ^ far], parts[j]) for j in range(len(parts))]
    return jnp.concatenate(parts)


def both_ways(block, x, y):
    rows, half = block.shape[0], block.shape[1] // 2
    a, b = block[:, :half], block[:, half:]
    a_theirs, b_theirs = swapped(a, y), swapped(b, x)
    a, b = in_order([a, a_theirs], [y]), in_order([b, b_theirs], [x])
    a_theirs, b_theirs = swapped(a, x), swapped(b, y)
    a, b = in_order([a, a_theirs], [x]), in_order([b, b_theirs], [y])
    b = b.reshape(2, 2, rows, half).transpose(1, 0, 2, 3).reshape(4 * rows, half)
    return jnp.concatenate([a, b], axis=1)


def products_kernel(low, mixed, d_branch, d_upper, d_att, active, made):
    step = pl.program_id(0)
    count = (pl.num_programs(0) - 1) // 2
    middle = (step >= count) & (step < 2 * count)
    for here, left, right in ((step < count, d_branch, active), (middle, low, d_upper), (step == 2 * count, mixed, d_att)):
        @pl.when(here)
        def _():
            made[...] = mm(left[...], right[...], NN).astype(BF16)


def feed_forward_products(low, mixed, d_branch, d_upper, d_att, active):
    d, rows = low.shape
    count = active.shape[1] // d
    once = lambda n, m: pl.BlockSpec((n, m), lambda j: (0, 0), pipeline_mode=pl.Buffered(1))
    along = lambda first: pl.BlockSpec((rows, d), lambda j: (0, jnp.clip(j - first, 0, count - 1)))
    return pl.pallas_call(
        products_kernel,
        grid=(2 * count + 1,),
        in_specs=[once(d, rows)] * 3 + [along(count), once(rows, d), along(0)],
        out_specs=pl.BlockSpec((d, d), lambda j: (0, j)),
        out_shape=jax.ShapeDtypeStruct((d, (2 * count + 1) * d), BF16),
        compiler_params=pltpu.CompilerParams(vmem_limit_bytes=VMEM),
        cost_estimate=pl.CostEstimate(flops=2 * rows * d * d * (2 * count + 1), bytes_accessed=20 * d * d * count,
                                      transcendentals=0),
        name="products",
    )(low, mixed, d_branch, d_upper, d_att, active)


def place_kernel(from_down, from_up, from_out, down, up, out):
    down[...] = from_down[...].T.astype(F32)
    up[...] = from_up[...].astype(F32)
    out[...] = from_out[...].astype(F32)


def feed_forward_whole(got):
    d = got.shape[0]
    ff = (got.shape[1] - d) // 2
    steps = d // PAIR
    row = lambda n: pl.BlockSpec((PAIR, n), lambda j: (j, 0))
    return pl.pallas_call(
        place_kernel,
        grid=(steps,),
        in_specs=[pl.BlockSpec((d, ff // steps), lambda j: (0, j)), pl.BlockSpec((PAIR, ff), lambda j: (j, 1)),
                  pl.BlockSpec((PAIR, d), lambda j: (j, 2 * ff // d))],
        out_specs=[pl.BlockSpec((ff // steps, d), lambda j: (j, 0)), row(ff), row(d)],
        out_shape=[jax.ShapeDtypeStruct(shape, F32) for shape in ((ff, d), (d, ff), (d, d))],
        compiler_params=pltpu.CompilerParams(vmem_limit_bytes=VMEM),
        cost_estimate=pl.CostEstimate(flops=0, bytes_accessed=12 * ff * d, transcendentals=0),
        name="place",
    )(got, got, got)


def split_kernel(x, q, k, v):
    for i, out in enumerate((q, k, v)):
        for p in range(q.shape[1] // PAIR):
            at = (3 * p + i) * PAIR
            out[:, p * PAIR:(p + 1) * PAIR] = x[:, at:at + PAIR].astype(F32)


def split_projections(x):
    d = x.shape[0]
    tr = d // 3
    row = lambda n: pl.BlockSpec((tr, n), lambda i: (i, 0))
    return pl.pallas_call(
        split_kernel,
        grid=(3,),
        in_specs=[row(3 * d)],
        out_specs=[row(d)] * 3,
        out_shape=[jax.ShapeDtypeStruct((d, d), F32)] * 3,
        compiler_params=pltpu.CompilerParams(vmem_limit_bytes=32 * 2**20),
        cost_estimate=pl.CostEstimate(flops=0, bytes_accessed=18 * d * d, transcendentals=0),
        name="split",
    )(x)


def tag_columns(page_ids, near_tags):
    place = jnp.arange(PAIR)[None, :] % HEAD
    qtag = jnp.where(jnp.arange(PAIR)[None, :] == page_ids[:, None], 1.0, 0.0).astype(BF16)
    ktag = jnp.where((place < 2) & (near_tags[:, None] != place + 1), BLOCKED, 0.0)
    return qtag, jnp.where((place >= 2) & (place < 5), -1.0, ktag).astype(BF16)


def tokens_of(near_tags, rows):
    have = jnp.sum((near_tags.reshape(-1, rows) > 0).astype(jnp.int32), axis=1)
    return (have + (TILE - 1)) // TILE


def tile_bits(tags, tile):
    tags = tags.reshape(-1, tile)
    return sum(jnp.max(jnp.where(tags == d + 1, 1 << d, 0), axis=1) for d in range(2)).astype(jnp.int32)


def body(hidden, page_ids, key_mask, out_grad, w_query, b_query, w_key, w_value, b_value, w_out, b_out, gain_one,
         shift_one, w_up, b_up, w_down, b_down, gain_two, shift_two):
    rows, d = hidden.shape
    bands = lax.axis_size("band")
    mates = [(i, i ^ 1) for i in range(bands)]
    across = [(i, i + 1) for i in range(1, bands - 1, 2)] + [(i + 1, i) for i in range(1, bands - 1, 2)]
    to_mate = lambda x: lax.ppermute(x, "band", mates)
    to_across = lambda x: lax.ppermute(x, "band", across)

    key_tags = jnp.where(key_mask == 1, page_ids + 1, 0)
    far, mate = to_across(hidden), to_mate(hidden)
    near_tags = jnp.concatenate([key_tags, to_mate(key_tags), to_across(key_tags)])
    queries, *own_pair = project(hidden, w_key, w_value, b_value, w_query, b_query)
    mate_pair, far_pair = project(mate, w_key, w_value, b_value), project(far, w_key, w_value, b_value)
    keys, values = zip(own_pair, mate_pair, far_pair)
    qtag, ktag = tag_columns(page_ids, near_tags)
    tk = 512
    tokens, qbits, kbits = tokens_of(near_tags, rows), tile_bits(key_tags, TILE), tile_bits(near_tags, tk)
    tokens, qbits, kbits, queries = lax.optimization_barrier((tokens, qbits, kbits, queries))

    mixed, ext = attend(queries, keys, values, qtag, ktag, tokens)
    (result, low_t, mixed_t, d_branch_t, active, d_upper, d_one, d_att, d_mixed, sums) = dense(
        hidden, mixed, out_grad, key_mask, w_out, w_up, w_down, b_out, gain_one, shift_one, b_up, b_down, gain_two,
        shift_two)

    count = everyone().bit_length() - 1
    core, y, x, z = 1, 2, bands, 2 * bands
    rest = [1 << i for i in range(count) if 1 << i not in (core, y, x, z)]
    direct = [[core], [x, y]] + [([z] + rest)[i:i + 2] for i in range(0, 1 + len(rest), 2)]

    products = feed_forward_products(low_t, mixed_t, d_branch_t, d_upper, d_att, active)
    products, d_mixed = lax.optimization_barrier((products, d_mixed))
    shares = lax.psum_scatter(products, ALL, scatter_dimension=0, tiled=True)

    pairs = d // PAIR
    kept, made, at, after = (sums,), [], 0, []
    for size in (2, 2, pairs - 4):
        *kept, made_now = attend_back(at, size, kept, after, queries, keys, values, d_mixed, mixed, ext, ktag,
                                      (hidden, mate, far), qbits, kbits, tk)
        at += size
        made.append(made_now)
        if at == 2:
            early = Summing(dealt(made[0], [core], 0), direct[:2])
            after = early.parts
        elif at == 4:
            kept[1] = early.advance(kept[1])
            late = Summing(dealt(made[1], [core], 0), direct[:1])
            after = early.parts + late.parts
    for stream in (early, late):
        kept[1] = stream.advance(kept[1])
    vectors, dq, dk, dv = kept

    keep, send = dealt(made[-1], [core], 0)
    vectors = vectors.astype(BF16)
    dk, send = lax.optimization_barrier((dk, send))
    theirs = [swapped(send, core), swapped(vectors, core)]
    far_part = back_product(2, dk, dv, w_key, w_value)
    theirs, far_part = lax.optimization_barrier((theirs, far_part))
    far_part = to_across(far_part)
    block = jnp.concatenate([late.parts[0], summed([keep, theirs[0]])], axis=1)
    vectors = summed([vectors, theirs[1]])
    vectors = jnp.concatenate([vectors[:8], vectors[8:]], axis=1)
    for i, bits in enumerate(direct[1:]):
        parts = dealt(block, bits, 0)
        send = [jnp.concatenate([part, vectors]) for part in parts[1:]]
        if i == 0:
            send, dk = lax.optimization_barrier((send, dk))
        theirs = sent(send, bits)
        if i == 0:
            shares, dk = lax.optimization_barrier((shares, dk))
            got = lax.all_gather(shares, ALL, axis=0, tiled=True)
            mate_part = back_product(1, dk, dv, w_key, w_value)
            theirs, mate_part = lax.optimization_barrier((theirs, mate_part))
            mate_part = to_mate(mate_part)
        elif i == 1:
            input_grad = back_product(0, dk, dv, w_key, w_value, (dq, w_query, d_one, mate_part, far_part))
            theirs, input_grad = lax.optimization_barrier((theirs, input_grad))
        size = parts[0].shape[0]
        block = summed([parts[0]] + [other[:size] for other in theirs])
        vectors = summed([vectors] + [other[size:] for other in theirs])
        if i == 0:
            block = jnp.concatenate([early.parts[0], block], axis=1)
            vectors = jnp.pad(vectors, ((0, 0), (0, block.shape[1] - vectors.shape[1])))
    vectors = jnp.concatenate([vectors[:, :d], vectors[:, d:2 * d]]).astype(F32)

    for bits in reversed(direct):
        if bits == [x, y]:
            block = both_ways(block, x, y)
            continue
        theirs = sent([block] * (len(masks_of(bits)) - 1), bits)
        block = in_order([block] + theirs, bits)
    grad_query, grad_key, grad_value = split_projections(block)
    got, grad_query = lax.optimization_barrier((got, grad_query))
    grad_down, grad_up, grad_out = feed_forward_whole(got)
    return (
        result,
        input_grad,
        grad_query,
        vectors[12],
        grad_key,
        grad_value,
        vectors[13],
        grad_out,
        vectors[5],
        vectors[3],
        vectors[4],
        grad_up,
        vectors[8:12].reshape(-1),
        grad_down,
        vectors[2],
        vectors[0],
        vectors[1],
    )


def solution(mesh):
    split = P(("page", "band"), None)
    line = P(("page", "band"))
    return jax.shard_map(
        body,
        mesh=mesh,
        in_specs=(split, line, line, split) + (P(),) * 15,
        out_specs=(split, split) + (P(),) * 15,
        check_vma=False,
    )
```
